256 devices in a mesh: seq: 64 (over x, z, core), ep: 4 (over y).
Axes of the slice: x: 4, y: 4, z: 8, core: 2. Of those that a mesh axis runs over, the one named last changes fastest.
Arguments:
- queries: bfloat16 [8192, 4096], P('seq', 'ep'), may hold values from -256 to 256
- keys: bfloat16 [8192, 512], P('seq', 'ep'), may hold values from -6 to 6
- values: bfloat16 [8192, 512], P('seq', 'ep'), may hold values from -6 to 6
- hidden: bfloat16 [8192, 2048], P('seq'), may hold values from -6 to 6
- cotangent: bfloat16 [8192, 2048], P('seq'), may hold values from -6 to 6
- routes: int32 [8192, 8], P('seq'), may hold values from 0 to 31, all different within a row; in each aligned block of 128 rows (0 to 127, 128 to 255, ...) at most 40 rows name the same one
- route_weight: float32 [8192, 8], P('seq'), may hold values from 0.2 to 1
- w_gate_up: bfloat16 [4, 64, 2048, 384], P('ep', 'seq'), may hold values from -0.125 to 0.125
- w_down: bfloat16 [4, 64, 192, 2048], P('ep', 'seq'), may hold values from -0.15625 to 0.15625
- adapter_in: bfloat16 [4, 64, 2048, 16], P('ep', 'seq'), may hold values from -0.125 to 0.125
- adapter_out: bfloat16 [4, 64, 64, 384], P('ep', 'seq'), may hold values from -0.75 to 0.75
Outputs:
- context: bfloat16 [8192, 4096], P('seq', 'ep')
- mixed: bfloat16 [8192, 2048], P('seq', 'ep')
- grad_adapter_in: float32 [4, 64, 2048, 16], P('ep', 'seq')
- grad_adapter_out: float32 [4, 64, 64, 384], P('ep', 'seq')
The draws below stay inside these ranges and needn't reach their ends.
Inputs may be any that keep to these rules, and one draw needn't show every extreme that they name: `routes`: among the 128 tokens of each seq index at most 40 pick any one expert, and 40 is reached; a token's 8 experts differ.
All inputs are finite; a program needn't handle non-finite values.
Results may differ from the reference program's by a relative error of at most 0.017.
Values may be sent and summed in bfloat16 or wider, within the bound.
A program may use at most 128 MiB of HBM per device.

```python
import math
import jax
import jax.numpy as jnp
import numpy as np
from jax import lax

D = 2048
QUERY_HEAD_COUNT = 32
KEY_VALUE_HEADS = 4
HEAD_WIDTH = 128
FF = 1536
TOP = 8
EXPERTS = 32
RANK = 64
TOK_SEQ = 128
TOKEN_COUNT = 8192
CAP = 40
GROUP = 8
FF_SH = 192
LOWR = 16
N_SEQ = 64
N_EP = 4


def shared_keys(key):
    return jnp.clip(jax.random.normal(key, (TOKEN_COUNT, KEY_VALUE_HEADS * HEAD_WIDTH), jnp.float32), -6.0, 6.0)


def draw_keys(key, part):
    base_offset = shared_keys(key)
    return base_offset.astype(jnp.bfloat16)


def draw_queries(key, part):
    key = jax.random.fold_in(key, 9)
    first_key = jax.random.fold_in(key, 0)
    result = jnp.clip(jax.random.normal(first_key, (TOKEN_COUNT, QUERY_HEAD_COUNT * HEAD_WIDTH), jnp.float32), -6.0, 6.0)
    return result.astype(jnp.bfloat16)


def shard_levels(key, dims, pieces, smallest, high):
    level, own = 1.0, jax.random.fold_in(key, 6)
    for dim, parts in pieces:
        steps = jnp.exp(jax.random.uniform(jax.random.fold_in(own, dim), (parts,), jnp.float32, smallest / len(pieces), high / len(pieces)))
        level = level * jnp.repeat(steps, dims[dim] // parts).reshape([-1 if axis == dim else 1 for axis in range(len(dims))])
    return level


def routed_block(key, own, number, rows, amount, top, most, skew):
    ranking = jax.random.permutation(key, amount)
    crowded, usual = portions_of(amount, rows * top, most, skew, True), portions_of(amount, rows * top, most, skew, False)
    places = jnp.arange(amount)

    def named(lengths, offset_by):
        used = int((lengths > 0).sum())
        fixed = max(1, used // 4)
        moved = fixed + (places - fixed + offset_by * (used - fixed)) % max(1, amount - fixed)
        return jnp.zeros((amount,), jnp.int32).at[ranking[jnp.where(places < fixed, places, moved)]].set(jnp.asarray(lengths, jnp.int32))

    lengths = jnp.where(number % 4 == 0, named(crowded, number // 4), named(usual, number - number // 4 - 1))
    mixed = jax.random.permutation(jax.random.fold_in(own, 3), amount)
    donor, receiver = mixed[0:amount // 2 * 2:2], mixed[1:amount // 2 * 2:2]
    slack = jnp.minimum(lengths[donor] - 1, most - lengths[receiver]) // 2
    slack = jnp.where((donor == ranking[0]) | (receiver == ranking[0]) | (lengths[receiver] == 0), 0, jnp.maximum(slack, 0))
    moved = jax.random.randint(jax.random.fold_in(own, 4), (amount // 2,), 0, 1 << 20) % (slack + 1)
    lengths = lengths.at[donor].add(-moved).at[receiver].add(moved)
    items = jnp.searchsorted(jnp.cumsum(lengths), jnp.arange(rows * top), side="right").astype(jnp.int32)
    listing = items.reshape(top, rows).T
    listing = listing[jax.random.permutation(jax.random.fold_in(own, 1), rows)]
    offset_by = jax.random.randint(jax.random.fold_in(own, 2), (rows, 1), 0, top)
    return jnp.take_along_axis(listing, (jnp.arange(top)[None, :] + offset_by) % top, axis=1)


def portions_of(amount, total, most, skew, full):
    weights = [(1 << 20) // math.isqrt(rank ** skew) + 1 for rank in range(1, amount + 1)]
    largest = most if full else min(most, max(-(-total // amount), total * weights[0] // sum(weights)))
    least = 1 if total - largest >= amount - 1 else 0
    counts, surplus = [largest] + [least] * (amount - 1), total - largest - least * (amount - 1)
    while surplus > 0:
        free = [i for i in range(1, amount) if counts[i] < largest] or [i for i in range(1, amount) if counts[i] < most]
        mass, remaining = sum([weights[i] for i in free]), surplus
        for i in free:
            addition = min(most - counts[i], max(1, remaining * weights[i] // mass), surplus)
            counts[i] = counts[i] + addition
            surplus = surplus - addition
    return np.array(counts)


def scatter_about(own_key, dims, deviation, limit, pieces=(), held_as=jnp.bfloat16):
    drawn = deviation * jax.random.normal(own_key, dims, jnp.float32)
    if pieces:
        drawn = drawn * shard_levels(own_key, dims, pieces, -0.22, 0.18)
    return jnp.clip(drawn, -limit, limit).astype(held_as)


def setup_inputs(seed: int = 0) -> dict:
    streams_of = jax.random.split(jax.random.key(seed), 12)
    queries = draw_queries(jax.random.fold_in(streams_of[11], 71), 0)
    keys = draw_keys(jax.random.fold_in(streams_of[11], 71), 0)
    values = scatter_about(streams_of[2], (TOKEN_COUNT, KEY_VALUE_HEADS * HEAD_WIDTH), 1.0, 6.0, ((0, 64), (1, 4)))
    hidden = scatter_about(streams_of[3], (TOKEN_COUNT, D), 1.0, 6.0, ((0, 64),))
    cotangent = scatter_about(streams_of[4], (TOKEN_COUNT, D), 1.0, 6.0, ((0, 64),))
    routes_keys = jax.random.split(jax.random.fold_in(streams_of[5], 1), TOKEN_COUNT // TOK_SEQ)
    routes_turns = jax.random.permutation(jax.random.fold_in(streams_of[5], 3), TOKEN_COUNT // TOK_SEQ)
    routes = jax.vmap(lambda own, number: routed_block(jax.random.fold_in(streams_of[5], 2), own, number, TOK_SEQ, EXPERTS, TOP, CAP, 2))(routes_keys, routes_turns).reshape((TOKEN_COUNT, TOP))
    route_weight = jnp.clip(0.2 + 0.8 * jax.random.uniform(streams_of[6], (TOKEN_COUNT, TOP), jnp.float32) ** shard_levels(streams_of[6], (TOKEN_COUNT, TOP), ((0, 64),), -0.2, 0.2), 0.2, 1.0)
    w_gate_up = scatter_about(streams_of[7], (N_EP, N_SEQ, D, 2 * FF_SH), D ** -0.5, 0.125, ((0, 4), (1, 64)))
    w_down = scatter_about(streams_of[8], (N_EP, N_SEQ, FF_SH, D), FF ** -0.5, 0.15625, ((0, 4), (1, 64)))
    adapter_in = scatter_about(streams_of[9], (N_EP, N_SEQ, D, LOWR), D ** -0.5, 0.125, ((0, 4), (1, 64)))
    adapter_out = scatter_about(streams_of[10], (N_EP, N_SEQ, RANK, 2 * FF_SH), RANK ** -0.5, 0.75, ((0, 4), (1, 64)))
    return dict(queries=queries, keys=keys, values=values, hidden=hidden, cotangent=cotangent, routes=routes, route_weight=route_weight, w_gate_up=w_gate_up, w_down=w_down, adapter_in=adapter_in, adapter_out=adapter_out)


def head_attention(inputs):
    query_rows, key_rows, value_rows = inputs
    scores = jnp.dot(query_rows, key_rows.T, preferred_element_type=jnp.float32) * (HEAD_WIDTH ** -0.5)
    positions = jnp.arange(TOKEN_COUNT, dtype=jnp.int32)
    allowed = positions[None, :] <= positions[:, None]
    masked = jnp.where(allowed, scores, -1e30)
    top_score = jnp.max(masked, axis=1, keepdims=True)
    weights = jnp.where(allowed, jnp.exp(masked - top_score), 0.0)
    denominator = jnp.sum(weights, axis=1, keepdims=True)
    numerator = jnp.dot(weights.astype(jnp.bfloat16), value_rows, preferred_element_type=jnp.float32)
    return (numerator / denominator).astype(jnp.bfloat16)


def reference(queries, keys, values, hidden, cotangent, routes, route_weight, w_gate_up, w_down, adapter_in, adapter_out):
    heads_per_group = QUERY_HEAD_COUNT // KEY_VALUE_HEADS
    query_heads = queries.reshape(TOKEN_COUNT, QUERY_HEAD_COUNT, HEAD_WIDTH).transpose(1, 0, 2)
    heads_of_keys = jnp.repeat(keys.reshape(TOKEN_COUNT, KEY_VALUE_HEADS, HEAD_WIDTH).transpose(1, 0, 2), heads_per_group, axis=0)
    heads_of_values = jnp.repeat(values.reshape(TOKEN_COUNT, KEY_VALUE_HEADS, HEAD_WIDTH).transpose(1, 0, 2), heads_per_group, axis=0)
    context_heads = lax.map(head_attention, (query_heads, heads_of_keys, heads_of_values))
    context = context_heads.transpose(1, 0, 2).reshape(TOKEN_COUNT, QUERY_HEAD_COUNT * HEAD_WIDTH)

    both_in = w_gate_up.reshape(EXPERTS, GROUP, D, 2, FF_SH).transpose(0, 3, 2, 1, 4).reshape(EXPERTS, 2, D, FF)
    down_all = w_down.reshape(EXPERTS, FF, D)
    low_in_all = adapter_in.reshape(EXPERTS, GROUP, D, LOWR).transpose(0, 2, 1, 3).reshape(EXPERTS, D, 2 * RANK)
    low_out_all = adapter_out.reshape(EXPERTS, GROUP, RANK, 2, FF_SH).transpose(0, 3, 2, 1, 4).reshape(EXPERTS, 2, RANK, FF)
    expert_ids = jnp.arange(EXPERTS, dtype=jnp.int32)
    picked = routes[:, :, None] == expert_ids[None, None, :]
    coef_all = jnp.sum(jnp.where(picked, route_weight[:, :, None], 0.0), axis=1)
    chosen_all = jnp.sum(picked.astype(jnp.int32), axis=1)
    cot_wide = cotangent.astype(jnp.float32)
    slot_total = N_SEQ * CAP
    token_ids = jnp.arange(TOKEN_COUNT, dtype=jnp.int32)

    def expert_step(mixed_sum, inputs):
        gate_w, up_w, down_w, low_in, low_gate, low_up, coef, chosen = inputs
        slot = jnp.cumsum(chosen) - 1
        target = jnp.where(chosen > 0, slot, slot_total).astype(jnp.int32)
        index = jnp.zeros((slot_total,), jnp.int32).at[target].set(token_ids, mode="drop")
        valid = jnp.zeros((slot_total,), coef.dtype).at[target].set(jnp.ones((TOKEN_COUNT,), coef.dtype), mode="drop")
        rows = hidden[index]
        row_coef = coef[index] * valid
        row_cot = cot_wide[index]
        low = jnp.dot(rows, low_in, preferred_element_type=jnp.float32).astype(jnp.bfloat16)
        pre_gate = jnp.dot(rows, gate_w, preferred_element_type=jnp.float32) + jnp.dot(low[:, :RANK], low_gate, preferred_element_type=jnp.float32)
        pre_up = jnp.dot(rows, up_w, preferred_element_type=jnp.float32) + jnp.dot(low[:, RANK:], low_up, preferred_element_type=jnp.float32)
        active = (jax.nn.silu(pre_gate) * pre_up).astype(jnp.bfloat16)
        expert_out = jnp.dot(active, down_w, preferred_element_type=jnp.float32)
        mixed_sum = mixed_sum.at[index].add(row_coef[:, None] * expert_out)
        scaled = (row_coef[:, None] * row_cot).astype(jnp.bfloat16)
        back_act = jnp.dot(scaled, down_w.T, preferred_element_type=jnp.float32)
        sigmoid_val = jax.nn.sigmoid(pre_gate)
        grad_gate = (back_act * pre_up * sigmoid_val * (1.0 + pre_gate * (1.0 - sigmoid_val))).astype(jnp.bfloat16)
        grad_up = (back_act * jax.nn.silu(pre_gate)).astype(jnp.bfloat16)
        grad_bg = jnp.dot(low[:, :RANK].T, grad_gate, preferred_element_type=jnp.float32)
        grad_bu = jnp.dot(low[:, RANK:].T, grad_up, preferred_element_type=jnp.float32)
        grad_low = jnp.concatenate([jnp.dot(grad_gate, low_gate.T, preferred_element_type=jnp.float32), jnp.dot(grad_up, low_up.T, preferred_element_type=jnp.float32)], axis=1).astype(jnp.bfloat16)
        grad_in = jnp.dot(rows.T, grad_low, preferred_element_type=jnp.float32)
        return mixed_sum, (grad_in, jnp.stack([grad_bg, grad_bu]))

    start_sum = jnp.zeros((TOKEN_COUNT, D), jnp.float32)
    inputs = (both_in[:, 0], both_in[:, 1], down_all, low_in_all, low_out_all[:, 0], low_out_all[:, 1], coef_all.T, chosen_all.T)
    mixed_sum, grads = lax.scan(expert_step, start_sum, inputs)
    grad_in_all, grad_out_all = grads
    grad_adapter_in = grad_in_all.reshape(EXPERTS, D, GROUP, LOWR).transpose(0, 2, 1, 3).reshape(N_EP, N_SEQ, D, LOWR)
    grad_adapter_out = grad_out_all.reshape(EXPERTS, 2, RANK, GROUP, FF_SH).transpose(0, 3, 2, 1, 4).reshape(N_EP, N_SEQ, RANK, 2 * FF_SH)
    return context, mixed_sum.astype(jnp.bfloat16), grad_adapter_in, grad_adapter_out
```

```python
import jax
import jax.numpy as jnp
from jax import lax
from jax.experimental import pallas as pl
from jax.experimental.pallas import tpu as pltpu
from jax.sharding import PartitionSpec as P

BF = jnp.bfloat16
F32 = jnp.float32
MESH = pl.DeviceIdType.MESH

TOK = 128
D = 2048
HD = 128
HEADS = 8
FF = 192
BLK = 80
MAIN = 32
ROWS = 160
NX, NZ = 4, 8
PARTS = 8
LOWR = 16
RANK = 64
KEYS = 512
PIECES = 5


def dot(a, b, ca, cb):
    return lax.dot_general(a, b, (((ca,), (cb,)), ((), ())), preferred_element_type=F32)


def attention_kernel(q_ref, kv_ref, out_ref, top_ref, sum_ref, acc_ref):
    s = lax.axis_index("seq")
    scale = HD**-0.5 * 1.4426950408889634
    top_ref[...] = jnp.full_like(top_ref, -1e30)
    sum_ref[...] = jnp.zeros_like(sum_ref)
    acc_ref[...] = jnp.zeros_like(acc_ref)

    def absorb(block, masked):
        rows = pl.ds(pl.multiple_of(block * KEYS, KEYS), KEYS)
        keys = kv_ref[rows, :HD]
        vals = kv_ref[rows, HD:]
        if masked:
            kpos = block * KEYS + lax.broadcasted_iota(jnp.int32, (TOK, KEYS), 1)
            qpos = s * TOK + lax.broadcasted_iota(jnp.int32, (TOK, KEYS), 0)
            allowed = kpos <= qpos
        for h in range(HEADS):
            sc = dot(q_ref[:, h * HD : (h + 1) * HD], keys, 1, 1)
            if masked:
                sc = jnp.where(allowed, sc, -1e30)
            old = top_ref[h]
            new = jnp.maximum(old, jnp.max(sc, axis=1, keepdims=True))
            factor = jnp.exp2((old - new) * scale)
            w = jnp.exp2((sc - new[:, :1]) * scale)
            part = w[:, :HD]
            for j in range(1, KEYS // HD):
                part = part + w[:, j * HD : (j + 1) * HD]
            sum_ref[h] = sum_ref[h] * factor + part
            acc_ref[h] = acc_ref[h] * factor + dot(w.astype(BF), vals, 1, 0)
            top_ref[h] = new

    full = s // (KEYS // TOK)

    @pl.loop(0, full)
    def _(block):
        absorb(block, False)

    absorb(full, True)
    for h in range(HEADS):
        total = jnp.sum(sum_ref[h], axis=1, keepdims=True)
        out_ref[:, h * HD : (h + 1) * HD] = (acc_ref[h] / total).astype(BF)


def attend(queries, kv):
    vm = pl.BlockSpec(memory_space=pltpu.VMEM)
    return pl.pallas_call(
        attention_kernel,
        out_shape=jax.ShapeDtypeStruct((TOK, HEADS * HD), BF),
        in_specs=[vm, vm],
        out_specs=vm,
        scratch_shapes=[pltpu.VMEM((HEADS, TOK, HD), F32)] * 3,
        compiler_params=pltpu.CompilerParams(vmem_limit_bytes=32 << 20),
        cost_estimate=pl.CostEstimate(
            flops=4 * TOK * HEADS * HD * 8192, bytes_accessed=5 << 20, transcendentals=8 << 20
        ),
        name="attention",
    )(queries, kv)


def expert_kernel(
    hid, cot, routes, rw, wgu, wd, ain, aout,
    mixed_o, gin_o, gout_o,
    WG, WD, WA, WB, WBB, PL_, PR_, CF, CFT, SL,
    sendb, rowsb, X, C, acc, low, glow, gin, gout,
    retb, outb, gins, gouts, ginr, goutr, accm, mixs, mixr,
    ws, wr, lw, rs, rr, os_, orr, gs, gr, ys, yr,
):
    s = lax.axis_index("seq")
    e = lax.axis_index("ep")
    x = s // 16
    z = lax.rem(s // 2, 8)
    c = lax.rem(s, 2)
    zh = z // 4
    lz = lax.rem(z, 4)
    site = jnp.logical_or(lz == 1, lz == 2)
    site_i = site.astype(jnp.int32)
    side = jnp.where(lz >= 2, 1, 0)
    step = jnp.where(lz >= 2, 1, -1)
    my_expert = x * 2 + zh

    def dev(xx, zz, cc):
        return ((xx * NZ + zz) * 2 + cc, e)

    def in_group(l, cc):
        return dev(x, zh * 4 + l, cc)

    q = lax.rem((z + 2) // 4, 2)

    def site_of(n):
        xx = n // 2
        zz2 = lax.rem(n, 2)
        l = jnp.where(zz2 == 0, 1 + q, 2 - q)
        zs = zz2 * 4 + l
        way = jnp.where(l == 1, -1, 1)
        i = lax.rem((z - zs) * way + 8, 8)
        return xx, zs, i

    def source_of(i, xx):
        zz = lax.rem(z + step * i + 8, 8)
        return xx, zz

    barrier = pltpu.get_barrier_semaphore()

    def greet(device):
        pl.semaphore_signal(barrier, inc=1, device_id=device, device_id_type=MESH)

    for d in range(1, 8):
        k = lax.rem(lz * 2 + c + d, 8)
        greet(in_group(k // 2, lax.rem(k, 2)))
    for d in range(1, 4):
        greet((s, lax.rem(e + d, 4)))

    @pl.loop(0, 8)
    def _(n):
        xx, zs, _i = site_of(n)

        @pl.when(jnp.logical_not(jnp.logical_and(site, n == my_expert)))
        def _():
            greet(dev(xx, zs, c))

    @pl.when(site)
    def _():
        @pl.loop(0, 16)
        def _(j):
            xx, zz = source_of(j // 4, lax.rem(j, 4))

            @pl.when(jnp.logical_not(jnp.logical_and(j // 4 == 0, xx == x)))
            def _():
                greet(dev(xx, zz, c))

    pl.semaphore_wait(barrier, 18 + 14 * site_i)

    def slot(k, p):
        if p == 0:
            return WG.at[k, pl.ds(0, D // 2)]
        if p == 1:
            return WG.at[k, pl.ds(D // 2, D // 2)]
        return (WD, WA, WB)[p - 2].at[k]

    def own(p):
        if p == 0:
            return wgu.at[pl.ds(0, D // 2)]
        if p == 1:
            return wgu.at[pl.ds(D // 2, D // 2)]
        return (wd, ain, aout)[p - 2]

    def wcopy(src, k, p, role, device):
        return pltpu.make_async_remote_copy(
            src_ref=src, dst_ref=slot(k, p), send_sem=ws.at[role, p], recv_sem=wr.at[k, p],
            device_id=device, device_id_type=MESH,
        )

    sibling = in_group(lz, 1 - c)
    inner = in_group(3 - lz, c)
    feed = in_group(1 + jnp.where(site, 1 - side, side), c)
    mine = lz * 2 + c
    outer_l = side * 3
    k_outer = outer_l * 2 + c
    k_inner = (3 - lz) * 2 + c
    k_far = (3 - outer_l) * 2 + c
    order = (2, 0, 1, 3, 4)

    for p in order:
        wcopy(own(p), mine, p, 0, feed).start()

    def local_w(p):
        return pltpu.make_async_copy(own(p), slot(mine, p), lw.at[p])

    @pl.when(site)
    def _():
        for p in order:
            wcopy(own(p), mine, p, 1, sibling).start()
        for p in order:
            local_w(p).start()

    lane = lax.broadcasted_iota(jnp.int32, (TOK, TOK), 1)
    sub = lax.broadcasted_iota(jnp.int32, (TOK, TOK), 0)
    ids = lane + e * 8
    chosen = jnp.zeros((TOK, TOK), F32)
    coef = jnp.zeros((TOK, TOK), F32)
    for j in range(8):
        hit = routes[:, j : j + 1] == ids
        chosen = chosen + jnp.where(hit, 1.0, 0.0)
        coef = coef + jnp.where(hit, rw[:, j : j + 1], 0.0)
    chosen_t = chosen.T
    before = jnp.where(sub < lane, 1.0, 0.0).astype(BF)
    slot_t = dot(chosen_t.astype(BF), before, 1, 0)
    SL[...] = jnp.where(chosen_t > 0.5, slot_t, 1000.0)
    CF[...] = coef
    CFT[...] = coef.T

    row = lax.broadcasted_iota(jnp.int32, (BLK, TOK), 0)
    tail = row >= 2 * MAIN
    first = jnp.where(tail, row - MAIN, row)
    is_l = jnp.logical_or(row < MAIN, jnp.logical_and(tail, row < 2 * MAIN + 8))
    is_r = jnp.logical_not(is_l)
    target_l = jnp.where(is_l, first, -1).astype(F32)
    target_r = jnp.where(is_r, jnp.where(tail, row - MAIN - 8, row - MAIN), -1).astype(F32)

    def row_copy(n, xx, zs, i):
        return pltpu.make_async_remote_copy(
            src_ref=sendb.at[n], dst_ref=rowsb.at[i, x], send_sem=rs.at[n], recv_sem=rr.at[i, x],
            device_id=dev(xx, zs, c), device_id_type=MESH,
        )

    def is_own(n):
        return jnp.logical_and(site, n == my_expert)

    @pl.loop(0, 8)
    def _(n):
        slots = SL[pl.ds(n, 1), :]
        p_l = jnp.where(slots == target_l, 1.0, 0.0)
        p_r = jnp.where(slots == target_r, 1.0, 0.0)
        coef_r = jnp.sum(p_r * CFT[pl.ds(n, 1), :], axis=1, keepdims=True)
        p_l = p_l.astype(BF)
        p_r = p_r.astype(BF)
        PL_[n] = p_l
        PR_[n] = p_r
        block = (dot(p_l, hid[...], 1, 0) + dot(p_r, cot[...], 1, 0) * coef_r).astype(BF)
        xx, zs, i = site_of(n)

        @pl.when(is_own(n))
        def _():
            rowsb[0, x] = block

        @pl.when(jnp.logical_not(is_own(n)))
        def _():
            sendb[n] = block
            row_copy(n, xx, zs, i).start()

    def arrived(k, p):
        wcopy(slot(k, p), k, p, 0, sibling).wait_recv()

    @pl.when(site)
    def _():
        for p in order:
            arrived(k_outer, p)
            wcopy(slot(k_outer, p), k_outer, p, 2, inner).start()
            wcopy(slot(k_outer, p), k_outer, p, 3, sibling).start()
        for p in order:
            arrived(k_inner, p)
            wcopy(slot(k_inner, p), k_inner, p, 4, sibling).start()
        for p in order:
            arrived(k_far, p)
            wcopy(slot(k_far, p), k_far, p, 5, sibling).start()
        for p in order:
            local_w(p).wait()

        @pl.loop(0, 4)
        def _(l):
            for p in order:
                arrived(l * 2 + 1 - c, p)

        lanes = lax.broadcasted_iota(jnp.int32, (RANK, 2 * FF), 1)
        gin[...] = jnp.zeros_like(gin)
        gout[...] = jnp.zeros_like(gout)

        @pl.loop(0, PARTS)
        def _(k):
            b = WB[k].astype(F32)
            WBB[k, pl.ds(0, RANK)] = jnp.where(lanes < FF, b, 0.0).astype(BF)
            WBB[k, pl.ds(RANK, RANK)] = jnp.where(lanes >= FF, b, 0.0).astype(BF)

        @pl.loop(0, 4)
        def _(i):
            @pl.loop(0, 4)
            def _(xx):
                @pl.when(jnp.logical_not(jnp.logical_and(i == 0, xx == x)))
                def _():
                    pltpu.make_async_remote_copy(
                        src_ref=rowsb.at[i, xx], dst_ref=rowsb.at[i, xx], send_sem=rs.at[0],
                        recv_sem=rr.at[i, xx], device_id=sibling, device_id_type=MESH,
                    ).wait_recv()

            for j in range(4):
                X[j * MAIN : (j + 1) * MAIN] = rowsb[i, j, 0:MAIN]
                C[j * MAIN : (j + 1) * MAIN] = rowsb[i, j, MAIN : 2 * MAIN]
            for j in range(2):
                t0 = rowsb[i, 2 * j, 2 * MAIN : BLK].astype(F32)
                t1 = rowsb[i, 2 * j + 1, 2 * MAIN : BLK].astype(F32)
                at = 4 * MAIN + 16 * j
                X[at : at + 16] = jnp.concatenate([t0[:8], t1[:8]], axis=0).astype(BF)
                C[at : at + 16] = jnp.concatenate([t0[8:], t1[8:]], axis=0).astype(BF)
            rows = X[...]
            low[...] = dot(rows, WA[...].reshape(PARTS * LOWR, D), 1, 1).astype(BF)
            glow[...] = jnp.zeros_like(glow)
            acc[...] = jnp.zeros_like(acc)

            @pl.loop(0, PARTS)
            def _(k):
                lo = low[...]
                pre = dot(X[...], WG[k], 1, 0) + dot(lo, WBB[k], 1, 0)
                g = pre[:, :FF]
                u = pre[:, FF:]
                back = dot(C[...], WD[k], 1, 1)
                sig = 1.0 / (1.0 + jnp.exp(-g))
                silu = g * sig
                acc[...] += dot((silu * u).astype(BF), WD[k], 1, 0)
                dg = back * u * sig * (1.0 + g * (1.0 - sig))
                du = back * silu
                dgu = jnp.concatenate([dg, du], axis=1).astype(BF)
                r = dot(lo, dgu, 0, 0)
                gout[k] += jnp.where(lanes < FF, r[:RANK], r[RANK:])
                glow[...] += dot(dgu, WBB[k], 1, 1)

            gin[...] += dot(glow[...].astype(BF), X[...], 0, 0)

            for j in range(4):
                xx, zz = source_of(i, j)
                a = acc[j * MAIN : (j + 1) * MAIN].astype(BF)
                t = acc[4 * MAIN + 8 * j : 4 * MAIN + 8 * j + 8]
                t = jnp.concatenate([t[:, : D // 2], t[:, D // 2 :]], axis=0).astype(BF)
                mine_too = jnp.logical_and(i == 0, x == j)

                @pl.when(mine_too)
                def _():
                    outb[my_expert, 0:MAIN] = a[:, : D // 2]
                    outb[my_expert, MAIN : 2 * MAIN] = a[:, D // 2 :]
                    outb[my_expert, 2 * MAIN : BLK] = t

                @pl.when(jnp.logical_not(mine_too))
                def _():
                    retb[i, j, 0:MAIN] = a[:, : D // 2]
                    retb[i, j, MAIN : 2 * MAIN] = a[:, D // 2 :]
                    retb[i, j, 2 * MAIN : BLK] = t
                    pltpu.make_async_remote_copy(
                        src_ref=retb.at[i, j], dst_ref=outb.at[my_expert], send_sem=os_.at[i, j],
                        recv_sem=orr.at[my_expert], device_id=dev(xx, zz, c), device_id_type=MESH,
                    ).start()

        here = side * 2 + c

        def grad_copies(k):
            device = in_group(k // 2, lax.rem(k, 2))
            return [
                pltpu.make_async_remote_copy(
                    src_ref=src.at[k], dst_ref=dst.at[here], send_sem=gs.at[k, p],
                    recv_sem=gr.at[here, p], device_id=device, device_id_type=MESH,
                )
                for p, (src, dst) in enumerate(((gins, ginr), (gouts, goutr)))
            ]

        gins[...] = gin[...].reshape(PARTS, LOWR, D).astype(BF)
        gouts[...] = gout[...].astype(BF)

        @pl.loop(0, PARTS)
        def _(k):
            @pl.when(k == mine)
            def _():
                ginr[here] = gins[k]
                goutr[here] = gouts[k]

            @pl.when(k != mine)
            def _():
                for copy in grad_copies(k):
                    copy.start()

    accm[...] = jnp.zeros_like(accm)

    @pl.loop(0, 8)
    def _(n):
        @pl.when(jnp.logical_not(is_own(n)))
        def _():
            pltpu.make_async_remote_copy(
                src_ref=outb.at[n], dst_ref=outb.at[n], send_sem=rs.at[0], recv_sem=orr.at[n],
                device_id=sibling, device_id_type=MESH,
            ).wait_recv()

        cf = jnp.sum(jnp.where(lane == n, CF[...], 0.0), axis=1, keepdims=True)
        block = outb[n]
        accm[:, : D // 2] += cf * dot(PL_[n], block, 0, 0)
        accm[:, D // 2 :] += cf * dot(PR_[n], block, 0, 0)

    def y_copy(d):
        to = lax.rem(e + d, 4)
        return pltpu.make_async_remote_copy(
            src_ref=mixs.at[to], dst_ref=mixr.at[d - 1], send_sem=ys.at[d - 1], recv_sem=yr.at[d - 1],
            device_id=(s, to), device_id_type=MESH,
        )

    for yy in range(4):
        mixs[yy] = accm[:, yy * 512 : (yy + 1) * 512].astype(BF)
    for d in (2, 1, 3):
        y_copy(d).start()

    for n in range(4):
        self_site = jnp.logical_and(site, n == side * 2 + c)

        @pl.when(jnp.logical_not(self_site))
        def _():
            for p, dst in enumerate((ginr, goutr)):
                pltpu.make_async_remote_copy(
                    src_ref=dst.at[n], dst_ref=dst.at[n], send_sem=rs.at[0], recv_sem=gr.at[n, p],
                    device_id=sibling, device_id_type=MESH,
                ).wait_recv()

    gin_o[...] = sum([ginr[n].astype(F32) for n in range(1, 4)], ginr[0].astype(F32))
    gout_o[...] = sum([goutr[n].astype(F32) for n in range(1, 4)], goutr[0].astype(F32))

    total = accm[:, pl.ds(pl.multiple_of(e * 512, 512), 512)]
    for d in range(1, 4):
        y_copy(d).wait_recv()
        total = total + mixr[d - 1].astype(F32)
    mixed_o[...] = total.astype(BF)

    for d in range(1, 4):
        y_copy(d).wait_send()
    for p in order:
        wcopy(own(p), mine, p, 0, feed).wait_send()

    @pl.loop(0, 8)
    def _(n):
        xx, zs, i = site_of(n)

        @pl.when(jnp.logical_not(is_own(n)))
        def _():
            row_copy(n, xx, zs, i).wait_send()

    @pl.when(site)
    def _():
        for p in order:
            wcopy(own(p), mine, p, 1, sibling).wait_send()
            for role in range(2, 6):
                wcopy(slot(mine, p), mine, p, role, sibling).wait_send()

        @pl.loop(0, 4)
        def _(i):
            @pl.loop(0, 4)
            def _(j):
                @pl.when(jnp.logical_not(jnp.logical_and(i == 0, x == j)))
                def _():
                    pltpu.make_async_remote_copy(
                        src_ref=retb.at[i, j], dst_ref=outb.at[0], send_sem=os_.at[i, j],
                        recv_sem=orr.at[0], device_id=sibling, device_id_type=MESH,
                    ).wait_send()

        @pl.loop(0, PARTS)
        def _(k):
            @pl.when(k != mine)
            def _():
                for p, src in enumerate((gins, gouts)):
                    pltpu.make_async_remote_copy(
                        src_ref=src.at[k], dst_ref=src.at[k], send_sem=gs.at[k, p],
                        recv_sem=gr.at[0, p], device_id=sibling, device_id_type=MESH,
                    ).wait_send()


def experts(hidden, cotangent, routes, route_weight, wgu, wd, ain, aout):
    vm = pl.BlockSpec(memory_space=pltpu.VMEM)
    hbm = pl.BlockSpec(memory_space=pl.ANY)
    dma = pltpu.SemaphoreType.DMA
    v = pltpu.VMEM
    return pl.pallas_call(
        expert_kernel,
        out_shape=(
            jax.ShapeDtypeStruct((TOK, 512), BF),
            jax.ShapeDtypeStruct((LOWR, D), F32),
            jax.ShapeDtypeStruct((RANK, 2 * FF), F32),
        ),
        in_specs=[vm, vm, vm, vm, hbm, hbm, hbm, hbm],
        out_specs=(vm, vm, vm),
        scratch_shapes=[
            v((PARTS, D, 2 * FF), BF),
            v((PARTS, FF, D), BF),
            v((PARTS, LOWR, D), BF),
            v((PARTS, RANK, 2 * FF), BF),
            v((PARTS, 2 * RANK, 2 * FF), BF),
            v((8, BLK, TOK), BF),
            v((8, BLK, TOK), BF),
            v((TOK, TOK), F32),
            v((TOK, TOK), F32),
            v((TOK, TOK), F32),
            v((8, BLK, D), BF),
            v((4, NX, BLK, D), BF),
            v((ROWS, D), BF),
            v((ROWS, D), BF),
            v((ROWS, D), F32),
            v((ROWS, 2 * RANK), BF),
            v((ROWS, 2 * RANK), F32),
            v((PARTS * LOWR, D), F32),
            v((PARTS, RANK, 2 * FF), F32),
            v((4, NX, BLK, D // 2), BF),
            v((8, BLK, D // 2), BF),
            v((PARTS, LOWR, D), BF),
            v((PARTS, RANK, 2 * FF), BF),
            v((4, LOWR, D), BF),
            v((4, RANK, 2 * FF), BF),
            v((TOK, D), F32),
            v((4, TOK, 512), BF),
            v((3, TOK, 512), BF),
            dma((6, PIECES)),
            dma((PARTS, PIECES)),
            dma((PIECES,)),
            dma((8,)),
            dma((4, NX)),
            dma((4, NX)),
            dma((8,)),
            dma((PARTS, 2)),
            dma((4, 2)),
            dma((3,)),
            dma((3,)),
        ],
        compiler_params=pltpu.CompilerParams(
            collective_id=0, has_side_effects=True, vmem_limit_bytes=60 << 20
        ),
        cost_estimate=pl.CostEstimate(
            flops=16 << 30, bytes_accessed=32 << 20, transcendentals=1 << 20
        ),
        name="experts",
    )(hidden, cotangent, routes, route_weight, wgu, wd, ain, aout)


def local(
    queries, keys, values, hidden, cotangent, routes, route_weight,
    w_gate_up, w_down, adapter_in, adapter_out,
):
    kv = lax.all_gather(jnp.concatenate([keys, values], axis=1), "seq", axis=0, tiled=True)
    mixed, gin, gout = experts(
        hidden, cotangent, routes, route_weight,
        w_gate_up[0, 0], w_down[0, 0], adapter_in[0, 0].T, adapter_out[0, 0],
    )
    context = attend(queries, kv)
    return (context, mixed, gin.T[None, None], gout[None, None])


def solution(mesh):
    return jax.shard_map(
        local,
        mesh=mesh,
        in_specs=(
            P("seq", "ep"),
            P("seq", "ep"),
            P("seq", "ep"),
            P("seq", None),
            P("seq", None),
            P("seq", None),
            P("seq", None),
            P("ep", "seq", None, None),
            P("ep", "seq", None, None),
            P("ep", "seq", None, None),
            P("ep", "seq", None, None),
        ),
        out_specs=(
            P("seq", "ep"),
            P("seq", "ep"),
            P("ep", "seq", None, None),
            P("ep", "seq", None, None),
        ),
        check_vma=False,
    )
```

```python
import jax
import jax.numpy as jnp
from jax import lax
from jax.experimental import pallas as pl
from jax.experimental.pallas import tpu as pltpu
from jax.sharding import PartitionSpec as P

BF = jnp.bfloat16
F32 = jnp.float32
MESH = pl.DeviceIdType.MESH

TOK = 128
D = 2048
HD = 128
HEADS = 8
FF = 192
BLK = 80
MAIN = 32
ROWS = 160
NX, NZ = 4, 8
PARTS = 8
LOWR = 16
RANK = 64
KEYS = 1024
SCALE = HD**-0.5 * 1.4426950408889634
PIECES = 5


def dot(a, b, ca, cb):
    return lax.dot_general(a, b, (((ca,), (cb,)), ((), ())), preferred_element_type=F32)


def kernel(
    queries, keys, values, hid, cot, routes, rw, wgu, wd, ain, aout,
    ctx_o, mixed_o, gin_o, gout_o,
    kvb, QT, top, den, num,
    WG, WD, WA, WB, WBB, PL_, PR_, CF, CFT, SL,
    sendb, rowsb, X, C, acc, low, glow, gin, gout,
    retb, outb, gins, gouts, ginr, goutr, accm, mixs, mixr,
    ws, wr, lw, rs, rr, os_, orr, gs, gr, ys, yr, kzs, kzr, kxs, kxr, kcs, kcr,
):
    s = lax.axis_index("seq")
    e = lax.axis_index("ep")
    x = s // 16
    z = lax.rem(s // 2, 8)
    c = lax.rem(s, 2)
    zh = z // 4
    lz = lax.rem(z, 4)
    site = jnp.logical_or(lz == 1, lz == 2)
    site_i = site.astype(jnp.int32)
    side = jnp.where(lz >= 2, 1, 0)
    step = jnp.where(lz >= 2, 1, -1)
    my_expert = x * 2 + zh

    def dev(xx, zz, cc):
        return ((xx * NZ + zz) * 2 + cc, e)

    def in_group(l, cc):
        return dev(x, zh * 4 + l, cc)

    q = lax.rem((z + 2) // 4, 2)

    def site_of(n):
        xx = n // 2
        zz2 = lax.rem(n, 2)
        l = jnp.where(zz2 == 0, 1 + q, 2 - q)
        zs = zz2 * 4 + l
        way = jnp.where(l == 1, -1, 1)
        i = lax.rem((z - zs) * way + 8, 8)
        return xx, zs, i

    def source_of(i, xx):
        zz = lax.rem(z + step * i + 8, 8)
        return xx, zz

    place = x * NZ + z
    kvb[place, c, :, 0:HD] = keys[...]
    kvb[place, c, :, HD:] = values[...]

    barrier = pltpu.get_barrier_semaphore()

    def greet(device):
        pl.semaphore_signal(barrier, inc=1, device_id=device, device_id_type=MESH)

    for d in range(1, 8):
        k = lax.rem(lz * 2 + c + d, 8)
        greet(in_group(k // 2, lax.rem(k, 2)))
    for d in range(1, 4):
        greet((s, lax.rem(e + d, 4)))
        greet(dev(lax.rem(x + d, 4), z, c))
    for d in range(1, 8):
        greet(dev(x, lax.rem(z + d, 8), c))

    @pl.loop(0, 8)
    def _(n):
        xx, zs, _i = site_of(n)

        @pl.when(jnp.logical_not(jnp.logical_and(site, n == my_expert)))
        def _():
            greet(dev(xx, zs, c))

    @pl.when(site)
    def _():
        @pl.loop(0, 16)
        def _(j):
            xx, zz = source_of(j // 4, lax.rem(j, 4))

            @pl.when(jnp.logical_not(jnp.logical_and(j // 4 == 0, xx == x)))
            def _():
                greet(dev(xx, zz, c))

    pl.semaphore_wait(barrier, 28 + 14 * site_i)

    def z_copy(d):
        block = kvb.at[place, c]
        return pltpu.make_async_remote_copy(
            src_ref=block, dst_ref=block, send_sem=kzs.at[d - 1], recv_sem=kzr.at[d - 1],
            device_id=dev(x, lax.rem(z + d, 8), c), device_id_type=MESH,
        )

    def x_copy(d):
        block = kvb.at[pl.ds(x * NZ, NZ), c]
        return pltpu.make_async_remote_copy(
            src_ref=block, dst_ref=block, send_sem=kxs.at[d - 1], recv_sem=kxr.at[d - 1],
            device_id=dev(lax.rem(x + d, 4), z, c), device_id_type=MESH,
        )

    def core_copy(d):
        block = kvb.at[pl.ds(lax.rem(x + 4 - d, 4) * NZ, NZ), c]
        return pltpu.make_async_remote_copy(
            src_ref=block, dst_ref=block, send_sem=kcs.at[d], recv_sem=kcr.at[d],
            device_id=dev(x, z, 1 - c), device_id_type=MESH,
        )

    for d in (4, 3, 5, 2, 6, 1, 7):
        z_copy(d).start()

    def slot(k, p):
        if p == 0:
            return WG.at[k, pl.ds(0, D // 2)]
        if p == 1:
            return WG.at[k, pl.ds(D // 2, D // 2)]
        return (WD, WA, WB)[p - 2].at[k]

    def own(p):
        if p == 0:
            return wgu.at[pl.ds(0, D // 2)]
        if p == 1:
            return wgu.at[pl.ds(D // 2, D // 2)]
        return (wd, ain, aout)[p - 2]

    def wcopy(src, k, p, role, device):
        return pltpu.make_async_remote_copy(
            src_ref=src, dst_ref=slot(k, p), send_sem=ws.at[role, p], recv_sem=wr.at[k, p],
            device_id=device, device_id_type=MESH,
        )

    sibling = in_group(lz, 1 - c)
    inner = in_group(3 - lz, c)
    feed = in_group(1 + jnp.where(site, 1 - side, side), c)
    mine = lz * 2 + c
    outer_l = side * 3
    k_outer = outer_l * 2 + c
    k_inner = (3 - lz) * 2 + c
    k_far = (3 - outer_l) * 2 + c
    order = (2, 0, 1, 3, 4)

    for p in order:
        wcopy(own(p), mine, p, 0, feed).start()

    def local_w(p):
        return pltpu.make_async_copy(own(p), slot(mine, p), lw.at[p])

    @pl.when(site)
    def _():
        for p in order:
            wcopy(own(p), mine, p, 1, sibling).start()
        for p in order:
            local_w(p).start()

    lane = lax.broadcasted_iota(jnp.int32, (TOK, TOK), 1)
    sub = lax.broadcasted_iota(jnp.int32, (TOK, TOK), 0)
    ids = sub + e * 8
    chosen = jnp.zeros((TOK, TOK), F32)
    coef = jnp.zeros((TOK, TOK), F32)
    for j in range(8):
        hit = routes[j : j + 1, :] == ids
        chosen = chosen + jnp.where(hit, 1.0, 0.0)
        coef = coef + jnp.where(hit, rw[j : j + 1, :], 0.0)
    before = jnp.where(sub < lane, 1.0, 0.0).astype(BF)
    slots_of = dot(chosen.astype(BF), before, 1, 0)
    SL[...] = jnp.where(chosen > 0.5, slots_of, 1000.0)
    CF[...] = coef.T
    CFT[...] = coef

    row = lax.broadcasted_iota(jnp.int32, (BLK, TOK), 0)
    tail = row >= 2 * MAIN
    first = jnp.where(tail, row - MAIN, row)
    is_l = jnp.logical_or(row < MAIN, jnp.logical_and(tail, row < 2 * MAIN + 8))
    is_r = jnp.logical_not(is_l)
    target_l = jnp.where(is_l, first, -1).astype(F32)
    target_r = jnp.where(is_r, jnp.where(tail, row - MAIN - 8, row - MAIN), -1).astype(F32)

    def row_copy(n, xx, zs, i):
        return pltpu.make_async_remote_copy(
            src_ref=sendb.at[n], dst_ref=rowsb.at[i, x], send_sem=rs.at[n], recv_sem=rr.at[i, x],
            device_id=dev(xx, zs, c), device_id_type=MESH,
        )

    def is_own(n):
        return jnp.logical_and(site, n == my_expert)

    @pl.loop(0, 8)
    def _(n):
        slots = SL[pl.ds(n, 1), :]
        p_l = jnp.where(slots == target_l, 1.0, 0.0)
        p_r = jnp.where(slots == target_r, 1.0, 0.0)
        coef_r = jnp.sum(p_r * CFT[pl.ds(n, 1), :], axis=1, keepdims=True)
        p_l = p_l.astype(BF)
        p_r = p_r.astype(BF)
        PL_[n] = p_l
        PR_[n] = p_r
        block = (dot(p_l, hid[...], 1, 0) + dot(p_r, cot[...], 1, 0) * coef_r).astype(BF)
        xx, zs, i = site_of(n)

        @pl.when(is_own(n))
        def _():
            rowsb[0, x] = block

        @pl.when(jnp.logical_not(is_own(n)))
        def _():
            sendb[n] = block

            @pl.when(i == 0)
            def _():
                row_copy(n, xx, zs, i).start()

    for d in range(1, 8):
        z_copy(d).wait_recv()
    for d in (2, 1, 3):
        x_copy(d).start()
    core_copy(0).start()
    for h in range(HEADS):
        QT[h] = queries[:, h * HD : (h + 1) * HD].astype(F32).T.astype(BF)
    top[...] = jnp.full_like(top, -1e30)
    den[...] = jnp.zeros_like(den)
    num[...] = jnp.zeros_like(num)
    for d in (1, 3, 2):
        x_copy(d).wait_recv()
        core_copy(d).start()
    for d in range(4):
        core_copy(d).wait_recv()

    def absorb(block, masked):
        kv = kvb[pl.ds(block * (KEYS // 256), KEYS // 256)]
        ks = kv[..., :HD].reshape(KEYS, HD)
        vs = kv[..., HD:].reshape(KEYS, HD)
        if masked:
            kpos = block * KEYS + lax.broadcasted_iota(jnp.int32, (KEYS, TOK), 0)
            qpos = s * TOK + lax.broadcasted_iota(jnp.int32, (KEYS, TOK), 1)
            allowed = kpos <= qpos
        for h in range(HEADS):
            sc = dot(ks, QT[h], 1, 0)
            if masked:
                sc = jnp.where(allowed, sc, -1e30)
            old = top[h, 0:1]
            new = jnp.maximum(old, jnp.max(sc, axis=0, keepdims=True))
            factor = jnp.exp2((old - new) * SCALE)
            w = jnp.exp2((sc - new) * SCALE)
            den[h, 0:1] = den[h, 0:1] * factor + jnp.sum(w, axis=0, keepdims=True)
            num[h] = num[h] * factor + dot(vs, w.astype(BF), 0, 0)
            top[h, 0:1] = new

    def arrived(k, p):
        wcopy(slot(k, p), k, p, 0, sibling).wait_recv()

    def from_outer(p):
        arrived(k_outer, p)
        wcopy(slot(k_outer, p), k_outer, p, 2, inner).start()
        wcopy(slot(k_outer, p), k_outer, p, 3, sibling).start()

    def from_inner(p):
        arrived(k_inner, p)
        wcopy(slot(k_inner, p), k_inner, p, 4, sibling).start()

    def from_far(p):
        arrived(k_far, p)
        wcopy(slot(k_far, p), k_far, p, 5, sibling).start()

    passing = [(f, ps) for f in (from_outer, from_inner, from_far) for ps in ((2,), (0,), (1, 3, 4))]
    full = s // (KEYS // TOK)

    @pl.loop(0, len(passing) - 1)
    def _(t):
        @pl.when(t < full)
        def _():
            absorb(t, False)

        for j, (f, ps) in enumerate(passing[:-1]):

            @pl.when(jnp.logical_and(site, t == j))
            def _():
                for p in ps:
                    f(p)

        @pl.when(t == 2)
        def _():
            @pl.when(jnp.logical_not(site))
            def _():
                for p in order:
                    wcopy(own(p), mine, p, 0, feed).wait_send()

            @pl.loop(0, 8)
            def _(n):
                xx, zs, i = site_of(n)

                @pl.when(jnp.logical_and(jnp.logical_not(is_own(n)), i > 0))
                def _():
                    row_copy(n, xx, zs, i).start()

    absorb(full, True)
    for h in range(HEADS):
        ctx_o[:, h * HD : (h + 1) * HD] = (num[h] / den[h, 0:1]).T.astype(BF)

    @pl.when(site)
    def _():
        for p in passing[-1][1]:
            from_far(p)
        for p in order:
            local_w(p).wait()

        @pl.loop(0, 4)
        def _(l):
            for p in order:
                arrived(l * 2 + 1 - c, p)

        lanes = lax.broadcasted_iota(jnp.int32, (RANK, 2 * FF), 1)
        gin[...] = jnp.zeros_like(gin)
        gout[...] = jnp.zeros_like(gout)

        @pl.loop(0, PARTS)
        def _(k):
            b = WB[k].astype(F32)
            WBB[k, pl.ds(0, RANK)] = jnp.where(lanes < FF, b, 0.0).astype(BF)
            WBB[k, pl.ds(RANK, RANK)] = jnp.where(lanes >= FF, b, 0.0).astype(BF)

        @pl.loop(0, 4)
        def _(i):
            @pl.loop(0, 4)
            def _(xx):
                @pl.when(jnp.logical_not(jnp.logical_and(i == 0, xx == x)))
                def _():
                    pltpu.make_async_remote_copy(
                        src_ref=rowsb.at[i, xx], dst_ref=rowsb.at[i, xx], send_sem=rs.at[0],
                        recv_sem=rr.at[i, xx], device_id=sibling, device_id_type=MESH,
                    ).wait_recv()

            for j in range(4):
                X[j * MAIN : (j + 1) * MAIN] = rowsb[i, j, 0:MAIN]
                C[j * MAIN : (j + 1) * MAIN] = rowsb[i, j, MAIN : 2 * MAIN]
            for j in range(2):
                t0 = rowsb[i, 2 * j, 2 * MAIN : BLK].astype(F32)
                t1 = rowsb[i, 2 * j + 1, 2 * MAIN : BLK].astype(F32)
                at = 4 * MAIN + 16 * j
                X[at : at + 16] = jnp.concatenate([t0[:8], t1[:8]], axis=0).astype(BF)
                C[at : at + 16] = jnp.concatenate([t0[8:], t1[8:]], axis=0).astype(BF)
            rows = X[...]
            low[...] = dot(rows, WA[...].reshape(PARTS * LOWR, D), 1, 1).astype(BF)
            glow[...] = jnp.zeros_like(glow)
            acc[...] = jnp.zeros_like(acc)

            @pl.loop(0, PARTS)
            def _(k):
                lo = low[...]
                pre = dot(X[...], WG[k], 1, 0) + dot(lo, WBB[k], 1, 0)
                g = pre[:, :FF]
                u = pre[:, FF:]
                back = dot(C[...], WD[k], 1, 1)
                sig = 1.0 / (1.0 + jnp.exp(-g))
                silu = g * sig
                acc[...] += dot((silu * u).astype(BF), WD[k], 1, 0)
                dg = back * u * sig * (1.0 + g * (1.0 - sig))
                du = back * silu
                dgu = jnp.concatenate([dg, du], axis=1).astype(BF)
                r = dot(lo, dgu, 0, 0)
                gout[k] += jnp.where(lanes < FF, r[:RANK], r[RANK:])
                glow[...] += dot(dgu, WBB[k], 1, 1)

            gin[...] += dot(glow[...].astype(BF), X[...], 0, 0)

            for j in range(4):
                xx, zz = source_of(i, j)
                a = acc[j * MAIN : (j + 1) * MAIN].astype(BF)
                t = acc[4 * MAIN + 8 * j : 4 * MAIN + 8 * j + 8]
                t = jnp.concatenate([t[:, : D // 2], t[:, D // 2 :]], axis=0).astype(BF)
                mine_too = jnp.logical_and(i == 0, x == j)

                @pl.when(mine_too)
                def _():
                    outb[my_expert, 0:MAIN] = a[:, : D // 2]
                    outb[my_expert, MAIN : 2 * MAIN] = a[:, D // 2 :]
                    outb[my_expert, 2 * MAIN : BLK] = t

                @pl.when(jnp.logical_not(mine_too))
                def _():
                    retb[i, j, 0:MAIN] = a[:, : D // 2]
                    retb[i, j, MAIN : 2 * MAIN] = a[:, D // 2 :]
                    retb[i, j, 2 * MAIN : BLK] = t
                    pltpu.make_async_remote_copy(
                        src_ref=retb.at[i, j], dst_ref=outb.at[my_expert], send_sem=os_.at[i, j],
                        recv_sem=orr.at[my_expert], device_id=dev(xx, zz, c), device_id_type=MESH,
                    ).start()

        here = side * 2 + c

        def grad_copies(k):
            device = in_group(k // 2, lax.rem(k, 2))
            return [
                pltpu.make_async_remote_copy(
                    src_ref=src.at[k], dst_ref=dst.at[here], send_sem=gs.at[k, p],
                    recv_sem=gr.at[here, p], device_id=device, device_id_type=MESH,
                )
                for p, (src, dst) in enumerate(((gins, ginr), (gouts, goutr)))
            ]

        gins[...] = gin[...].reshape(PARTS, LOWR, D).astype(BF)
        gouts[...] = gout[...].astype(BF)

        @pl.loop(0, PARTS)
        def _(k):
            @pl.when(k == mine)
            def _():
                ginr[here] = gins[k]
                goutr[here] = gouts[k]

            @pl.when(k != mine)
            def _():
                for copy in grad_copies(k):
                    copy.start()

    accm[...] = jnp.zeros_like(accm)

    @pl.loop(0, 8)
    def _(n):
        @pl.when(jnp.logical_not(is_own(n)))
        def _():
            pltpu.make_async_remote_copy(
                src_ref=outb.at[n], dst_ref=outb.at[n], send_sem=rs.at[0], recv_sem=orr.at[n],
                device_id=sibling, device_id_type=MESH,
            ).wait_recv()

        cf = jnp.sum(jnp.where(lane == n, CF[...], 0.0), axis=1, keepdims=True)
        block = outb[n]
        accm[:, : D // 2] += cf * dot(PL_[n], block, 0, 0)
        accm[:, D // 2 :] += cf * dot(PR_[n], block, 0, 0)

    def y_copy(d):
        to = lax.rem(e + d, 4)
        return pltpu.make_async_remote_copy(
            src_ref=mixs.at[to], dst_ref=mixr.at[d - 1], send_sem=ys.at[d - 1], recv_sem=yr.at[d - 1],
            device_id=(s, to), device_id_type=MESH,
        )

    for yy in range(4):
        mixs[yy] = accm[:, yy * 512 : (yy + 1) * 512].astype(BF)
    for d in (2, 1, 3):
        y_copy(d).start()

    for n in range(4):
        self_site = jnp.logical_and(site, n == side * 2 + c)

        @pl.when(jnp.logical_not(self_site))
        def _():
            for p, dst in enumerate((ginr, goutr)):
                pltpu.make_async_remote_copy(
                    src_ref=dst.at[n], dst_ref=dst.at[n], send_sem=rs.at[0], recv_sem=gr.at[n, p],
                    device_id=sibling, device_id_type=MESH,
                ).wait_recv()

    gin_o[...] = sum([ginr[n].astype(F32) for n in range(1, 4)], ginr[0].astype(F32))
    gout_o[...] = sum([goutr[n].astype(F32) for n in range(1, 4)], goutr[0].astype(F32))

    total = accm[:, pl.ds(pl.multiple_of(e * 512, 512), 512)]
    for d in range(1, 4):
        y_copy(d).wait_recv()
        total = total + mixr[d - 1].astype(F32)
    mixed_o[...] = total.astype(BF)

    for d in range(1, 4):
        y_copy(d).wait_send()
    for d in range(1, 8):
        z_copy(d).wait_send()
    for d in range(1, 4):
        x_copy(d).wait_send()
    for d in range(4):
        core_copy(d).wait_send()

    @pl.loop(0, 8)
    def _(n):
        xx, zs, i = site_of(n)

        @pl.when(jnp.logical_not(is_own(n)))
        def _():
            row_copy(n, xx, zs, i).wait_send()

    @pl.when(site)
    def _():
        for p in order:
            wcopy(own(p), mine, p, 0, feed).wait_send()
            wcopy(own(p), mine, p, 1, sibling).wait_send()
            for role in range(2, 6):
                wcopy(slot(mine, p), mine, p, role, sibling).wait_send()

        @pl.loop(0, 4)
        def _(i):
            @pl.loop(0, 4)
            def _(j):
                @pl.when(jnp.logical_not(jnp.logical_and(i == 0, x == j)))
                def _():
                    pltpu.make_async_remote_copy(
                        src_ref=retb.at[i, j], dst_ref=outb.at[0], send_sem=os_.at[i, j],
                        recv_sem=orr.at[0], device_id=sibling, device_id_type=MESH,
                    ).wait_send()

        @pl.loop(0, PARTS)
        def _(k):
            @pl.when(k != mine)
            def _():
                for p, src in enumerate((gins, gouts)):
                    pltpu.make_async_remote_copy(
                        src_ref=src.at[k], dst_ref=src.at[k], send_sem=gs.at[k, p],
                        recv_sem=gr.at[0, p], device_id=sibling, device_id_type=MESH,
                    ).wait_send()


def run(queries, keys, values, hidden, cotangent, routes, route_weight, wgu, wd, ain, aout):
    vm = pl.BlockSpec(memory_space=pltpu.VMEM)
    hbm = pl.BlockSpec(memory_space=pl.ANY)
    dma = pltpu.SemaphoreType.DMA
    v = pltpu.VMEM
    return pl.pallas_call(
        kernel,
        out_shape=(
            jax.ShapeDtypeStruct((TOK, HEADS * HD), BF),
            jax.ShapeDtypeStruct((TOK, 512), BF),
            jax.ShapeDtypeStruct((LOWR, D), F32),
            jax.ShapeDtypeStruct((RANK, 2 * FF), F32),
        ),
        in_specs=[vm] * 7 + [hbm] * 4,
        out_specs=(vm,) * 4,
        scratch_shapes=[
            v((NX * NZ, 2, TOK, 2 * HD), BF),
            v((HEADS, HD, TOK), BF),
            v((HEADS, 8, TOK), F32),
            v((HEADS, 8, TOK), F32),
            v((HEADS, HD, TOK), F32),
            v((PARTS, D, 2 * FF), BF),
            v((PARTS, FF, D), BF),
            v((PARTS, LOWR, D), BF),
            v((PARTS, RANK, 2 * FF), BF),
            v((PARTS, 2 * RANK, 2 * FF), BF),
            v((8, BLK, TOK), BF),
            v((8, BLK, TOK), BF),
            v((TOK, TOK), F32),
            v((TOK, TOK), F32),
            v((TOK, TOK), F32),
            v((8, BLK, D), BF),
            v((4, NX, BLK, D), BF),
            v((ROWS, D), BF),
            v((ROWS, D), BF),
            v((ROWS, D), F32),
            v((ROWS, 2 * RANK), BF),
            v((ROWS, 2 * RANK), F32),
            v((PARTS * LOWR, D), F32),
            v((PARTS, RANK, 2 * FF), F32),
            v((4, NX, BLK, D // 2), BF),
            v((8, BLK, D // 2), BF),
            v((PARTS, LOWR, D), BF),
            v((PARTS, RANK, 2 * FF), BF),
            v((4, LOWR, D), BF),
            v((4, RANK, 2 * FF), BF),
            v((TOK, D), F32),
            v((4, TOK, 512), BF),
            v((3, TOK, 512), BF),
            dma((6, PIECES)),
            dma((PARTS, PIECES)),
            dma((PIECES,)),
            dma((8,)),
            dma((4, NX)),
            dma((4, NX)),
            dma((8,)),
            dma((PARTS, 2)),
            dma((4, 2)),
            dma((3,)),
            dma((3,)),
            dma((7,)),
            dma((7,)),
            dma((3,)),
            dma((3,)),
            dma((4,)),
            dma((4,)),
        ],
        compiler_params=pltpu.CompilerParams(
            collective_id=0, has_side_effects=True, vmem_limit_bytes=60 << 20
        ),
        cost_estimate=pl.CostEstimate(
            flops=16 << 30, bytes_accessed=32 << 20, transcendentals=1 << 20
        ),
        name="whole",
    )(queries, keys, values, hidden, cotangent, routes, route_weight, wgu, wd, ain, aout)


def local(
    queries, keys, values, hidden, cotangent, routes, route_weight,
    w_gate_up, w_down, adapter_in, adapter_out,
):
    context, mixed, gin, gout = run(
        queries, keys, values, hidden, cotangent, routes.T, route_weight.T,
        w_gate_up[0, 0], w_down[0, 0], adapter_in[0, 0].T, adapter_out[0, 0],
    )
    return (context, mixed, gin.T[None, None], gout[None, None])


def solution(mesh):
    return jax.shard_map(
        local,
        mesh=mesh,
        in_specs=(
            P("seq", "ep"),
            P("seq", "ep"),
            P("seq", "ep"),
            P("seq", None),
            P("seq", None),
            P("seq", None),
            P("seq", None),
            P("ep", "seq", None, None),
            P("ep", "seq", None, None),
            P("ep", "seq", None, None),
            P("ep", "seq", None, None),
        ),
        out_specs=(
            P("seq", "ep"),
            P("seq", "ep"),
            P("ep", "seq", None, None),
            P("ep", "seq", None, None),
        ),
        check_vma=False,
    )
```

```python
import jax
import jax.numpy as jnp
from jax import lax
from jax.experimental import pallas as pl
from jax.experimental.pallas import tpu as pltpu
from jax.sharding import PartitionSpec as P

BF = jnp.bfloat16
F32 = jnp.float32
MESH = pl.DeviceIdType.MESH

TOK = 128
D = 2048
HD = 128
HEADS = 8
FF = 192
BLK = 80
MAIN = 32
ROWS = 160
NX, NZ = 4, 8
PARTS = 8
LOWR = 16
RANK = 64
KEYS = 1024
SCALE = HD**-0.5 * 1.4426950408889634
PIECES = 4
HALF = 4
OFF = (0, 2, 6, 4)


def dot(a, b, ca, cb):
    return lax.dot_general(a, b, (((ca,), (cb,)), ((), ())), preferred_element_type=F32)


def kernel(
    queries, keys, values, hid, cot, routes, rw, wgu, wd, ain, aout,
    ctx_o, mixed_o, gin_o, gout_o,
    kvb, QT, top, den, num, WG, WD, WA, WB, WBB, PL_, PR_, info, pk, tk,
    sendb, rowsb, X, C, acc, low, glow, gin, gout,
    retb, outb, gins, gouts, ginr, goutr, accm, accown, mixs, mixr, zsb, zrb,
    ws, wr, lw, was, war, rs, rr, os_, orr, gs, gr, hs, hr, ys, yr, zs, zr,
    tzs, tzr, tys, tyr, izs, izr, kzs, kzr, kxs, kxr, kcs, kcr,
):
    s = lax.axis_index("seq")
    e = lax.axis_index("ep")
    x = s // 16
    z = lax.rem(s // 2, 8)
    c = lax.rem(s, 2)
    zh = z // 4
    lz = lax.rem(z, 4)
    pair = lz // 2
    place = x * NZ + z
    mine = lz * 2 + c
    mine4 = lax.rem(lz, 2) * 2 + c

    def dev(xx, zz, cc):
        return ((xx * NZ + zz) * 2 + cc, e)

    def in_group(k):
        return dev(x, zh * 4 + k // 2, lax.rem(k, 2))

    def at_z(d):
        return dev(x, lax.rem(z + d, 8), c)

    def at_x(d):
        return dev(lax.rem(x + d, 4), z, c)

    def at_y(d):
        return (s, lax.rem(e + d, 4))

    sibling = dev(x, z, 1 - c)
    neighbour = dev(x, z + 1 - 2 * lax.rem(lz, 2), c)

    def remote(src, dst, send, recv, device):
        return pltpu.make_async_remote_copy(
            src_ref=src, dst_ref=dst, send_sem=send, recv_sem=recv, device_id=device, device_id_type=MESH
        )

    kvb[place, c, :, 0:HD] = keys[...]
    kvb[place, c, :, HD:] = values[...]
    quarter = pl.ds(pl.multiple_of(e * 32, 32), 32)
    pk[0:32] = hid[quarter, :]
    pk[32:64] = cot[quarter, :]
    lane = lax.broadcasted_iota(jnp.int32, (TOK, TOK), 1)
    sub = lax.broadcasted_iota(jnp.int32, (TOK, TOK), 0)
    ids = lax.broadcasted_iota(jnp.int32, (32, TOK), 0)
    chosen = jnp.zeros((32, TOK), F32)
    coef = jnp.zeros((32, TOK), F32)
    for j in range(8):
        hit = routes[j : j + 1, :] == ids
        chosen = chosen + jnp.where(hit, 1.0, 0.0)
        coef = coef + jnp.where(hit, rw[j : j + 1, :], 0.0)
    before = jnp.where(sub < lane, 1.0, 0.0).astype(BF)
    info[0, 0:32] = jnp.where(chosen > 0.5, dot(chosen.astype(BF), before, 1, 0), 1000.0)
    info[0, 32:64] = coef

    barrier = pltpu.get_barrier_semaphore()

    def greet(device):
        pl.semaphore_signal(barrier, inc=1, device_id=device, device_id_type=MESH)

    for d in range(1, 8):
        greet(at_z(d))
        greet(in_group(lax.rem(mine + d, 8)))
    for d in range(1, 4):
        greet(at_x(d))
        greet(at_y(d))
    pl.semaphore_wait(barrier, 20)

    def kz_copy(d):
        block = kvb.at[place, c]
        return remote(block, block, kzs.at[d - 1], kzr.at[d - 1], at_z(d))

    def kx_copy(d):
        block = kvb.at[pl.ds(x * NZ, NZ), c]
        return remote(block, block, kxs.at[d - 1], kxr.at[d - 1], at_x(d))

    def kc_copy(d):
        block = kvb.at[pl.ds(lax.rem(x + 4 - d, 4) * NZ, NZ), c]
        return remote(block, block, kcs.at[d], kcr.at[d], sibling)

    def tz_copy(j):
        return remote(pk, tk.at[j - 1, e], tzs.at[j - 1], tzr.at[j - 1], at_z(8 - OFF[j]))

    def ty_copy(j, d):
        block = tk.at[j - 1, e]
        return remote(block, block, tys.at[j - 1, d - 1], tyr.at[j - 1, d - 1], at_y(d))

    def info_copy(j):
        return remote(info.at[0], info.at[j], izs.at[j - 1], izr.at[j - 1], at_z(8 - OFF[j]))

    def slot(k, p):
        if p < 2:
            return WG.at[k, pl.ds(p * (D // 2), D // 2)]
        return (WD, WB)[p - 2].at[k]

    def own(p):
        if p < 2:
            return wgu.at[pl.ds(p * (D // 2), D // 2)]
        return (wd, aout)[p - 2]

    def w_copy(src, k, p, role, device):
        return remote(src, slot(k, p), ws.at[role, p], wr.at[k, p], device)

    def local_w(p):
        return pltpu.make_async_copy(own(p), slot(mine4, p), lw.at[p])

    def wa_copy(d):
        k = lax.rem(mine + d, 8)
        return remote(ain, WA.at[mine], was.at[d - 1], war.at[d - 1], in_group(k))

    local_wa = pltpu.make_async_copy(ain, WA.at[mine], lw.at[PIECES])
    near4 = lax.rem(mine4 + 2, 4)

    for j in (1, 2, 3):
        info_copy(j).start()
        tz_copy(j).start()
    for d in (4, 3, 5, 2, 6, 1, 7):
        kz_copy(d).start()
    for p in range(PIECES):
        w_copy(own(p), mine4, p, 0, neighbour).start()
    for p in range(PIECES):
        w_copy(own(p), mine4, p, 1, sibling).start()
        local_w(p).start()
    for d in range(1, 8):
        wa_copy(d).start()
    local_wa.start()

    row = lax.broadcasted_iota(jnp.int32, (BLK, TOK), 0)
    tail = row >= 2 * MAIN
    is_l = jnp.logical_or(row < MAIN, jnp.logical_and(tail, row < 2 * MAIN + 8))
    first = jnp.where(tail, row - MAIN, row)
    target_l = jnp.where(is_l, first, -1).astype(F32)
    target_r = jnp.where(is_l, -1, jnp.where(tail, row - MAIN - 8, row - MAIN)).astype(F32)

    def row_copy(j, n):
        return remote(sendb.at[j, n], rowsb.at[j, x], rs.at[j, n], rr.at[j, x], dev(n, z, c))

    def dispatch(j, h, g):
        @pl.loop(0, NX)
        def _(n):
            expert = e * 8 + n * 2 + zh
            slots = info[j, pl.ds(expert, 1), :]
            p_l = jnp.where(slots == target_l, 1.0, 0.0)
            p_r = jnp.where(slots == target_r, 1.0, 0.0)
            coef_r = jnp.sum(p_r * info[j, pl.ds(32 + expert, 1), :], axis=1, keepdims=True)
            p_l = p_l.astype(BF)
            p_r = p_r.astype(BF)
            PL_[j, n] = p_l
            PR_[j, n] = p_r
            block = (dot(p_l, h(), 1, 0) + dot(p_r, g(), 1, 0) * coef_r).astype(BF)

            @pl.when(n == x)
            def _():
                rowsb[j, n] = block

            @pl.when(n != x)
            def _():
                sendb[j, n] = block
                row_copy(j, n).start()

    dispatch(0, lambda: hid[...], lambda: cot[...])

    for j in (1, 2, 3):
        tz_copy(j).wait_recv()
        for d in (2, 1, 3):
            ty_copy(j, d).start()
    for d in range(1, 8):
        kz_copy(d).wait_recv()
    for d in (2, 1, 3):
        kx_copy(d).start()
    kc_copy(0).start()
    for h in range(HEADS):
        QT[h] = queries[:, h * HD : (h + 1) * HD].astype(F32).T.astype(BF)
    top[...] = jnp.full_like(top, -1e30)
    den[...] = jnp.zeros_like(den)
    num[...] = jnp.zeros_like(num)
    gin[...] = jnp.zeros_like(gin)
    gout[...] = jnp.zeros_like(gout)

    for j in (1, 2, 3):
        info_copy(j).wait_recv()

    @pl.loop(1, 4)
    def _(j):
        for d in (1, 3, 2):
            block = tk.at[j - 1, e]
            remote(block, block, tys.at[j - 1, d - 1], tyr.at[j - 1, d - 1], sibling).wait_recv()
        dispatch(
            j,
            lambda: tk[j - 1, :, 0:32].reshape(TOK, D),
            lambda: tk[j - 1, :, 32:64].reshape(TOK, D),
        )

    for d in (1, 3, 2):
        kx_copy(d).wait_recv()
        kc_copy(d).start()
    for d in range(4):
        kc_copy(d).wait_recv()

    def absorb(block, masked):
        kv = kvb[pl.ds(block * (KEYS // 256), KEYS // 256)]
        ks = kv[..., :HD].reshape(KEYS, HD)
        vs = kv[..., HD:].reshape(KEYS, HD)
        if masked:
            kpos = block * KEYS + lax.broadcasted_iota(jnp.int32, (KEYS, TOK), 0)
            qpos = s * TOK + lax.broadcasted_iota(jnp.int32, (KEYS, TOK), 1)
            allowed = kpos <= qpos
        for h in range(HEADS):
            sc = dot(ks, QT[h], 1, 0)
            if masked:
                sc = jnp.where(allowed, sc, -1e30)
            old = top[h, 0:1]
            new = jnp.maximum(old, jnp.max(sc, axis=0, keepdims=True))
            factor = jnp.exp2((old - new) * SCALE)
            w = jnp.exp2((sc - new) * SCALE)
            den[h, 0:1] = den[h, 0:1] * factor + jnp.sum(w, axis=0, keepdims=True)
            num[h] = num[h] * factor + dot(vs, w.astype(BF), 0, 0)
            top[h, 0:1] = new

    full = s // (KEYS // TOK)

    @pl.loop(0, full)
    def _(t):
        absorb(t, False)

    absorb(full, True)
    for h in range(HEADS):
        ctx_o[:, h * HD : (h + 1) * HD] = (num[h] / den[h, 0:1]).T.astype(BF)

    for p in range(PIECES):
        w_copy(slot(near4, p), near4, p, 0, sibling).wait_recv()
        w_copy(slot(near4, p), near4, p, 2, sibling).start()
    for d in range(1, 8):
        wa_copy(d).wait_recv()
    local_wa.wait()
    for p in range(PIECES):
        local_w(p).wait()
        for l in range(2):
            k = 2 * l + 1 - c
            w_copy(slot(k, p), k, p, 0, sibling).wait_recv()

    lanes = lax.broadcasted_iota(jnp.int32, (RANK, 2 * FF), 1)

    @pl.loop(0, HALF)
    def _(k):
        b = WB[k].astype(F32)
        WBB[k, pl.ds(0, RANK)] = jnp.where(lanes < FF, b, 0.0).astype(BF)
        WBB[k, pl.ds(RANK, RANK)] = jnp.where(lanes >= FF, b, 0.0).astype(BF)

    def work(i):
        for j in range(4):
            X[j * MAIN : (j + 1) * MAIN] = rowsb[i, j, 0:MAIN]
            C[j * MAIN : (j + 1) * MAIN] = rowsb[i, j, MAIN : 2 * MAIN]
        for j in range(2):
            t0 = rowsb[i, 2 * j, 2 * MAIN : BLK].astype(F32)
            t1 = rowsb[i, 2 * j + 1, 2 * MAIN : BLK].astype(F32)
            at = 4 * MAIN + 16 * j
            X[at : at + 16] = jnp.concatenate([t0[:8], t1[:8]], axis=0).astype(BF)
            C[at : at + 16] = jnp.concatenate([t0[8:], t1[8:]], axis=0).astype(BF)
        low[...] = dot(X[...], WA[...].reshape(PARTS * LOWR, D), 1, 1).astype(BF)
        glow[...] = jnp.zeros_like(glow)
        acc[...] = jnp.zeros_like(acc)

        @pl.loop(0, HALF)
        def _(k):
            lo = low[...]
            pre = dot(X[...], WG[k], 1, 0) + dot(lo, WBB[k], 1, 0)
            g = pre[:, :FF]
            u = pre[:, FF:]
            back = dot(C[...], WD[k], 1, 1)
            sig = 1.0 / (1.0 + jnp.exp(-g))
            silu = g * sig
            acc[...] += dot((silu * u).astype(BF), WD[k], 1, 0)
            dg = back * u * sig * (1.0 + g * (1.0 - sig))
            du = back * silu
            dgu = jnp.concatenate([dg, du], axis=1).astype(BF)
            r = dot(lo, dgu, 0, 0)
            gout[k] += jnp.where(lanes < FF, r[:RANK], r[RANK:])
            glow[...] += dot(dgu, WBB[k], 1, 1)

        for j in range(4):
            a = acc[j * MAIN : (j + 1) * MAIN].astype(BF)
            t = acc[4 * MAIN + 8 * j : 4 * MAIN + 8 * j + 8]
            t = jnp.concatenate([t[:, : D // 2], t[:, D // 2 :]], axis=0).astype(BF)

            @pl.when(x == j)
            def _():
                outb[i, j, 0:MAIN] = a[:, : D // 2]
                outb[i, j, MAIN : 2 * MAIN] = a[:, D // 2 :]
                outb[i, j, 2 * MAIN : BLK] = t

            @pl.when(x != j)
            def _():
                retb[i, j, 0:MAIN] = a[:, : D // 2]
                retb[i, j, MAIN : 2 * MAIN] = a[:, D // 2 :]
                retb[i, j, 2 * MAIN : BLK] = t
                remote(retb.at[i, j], outb.at[i, x], os_.at[i, j], orr.at[i, x], dev(j, z, c)).start()

        gin[...] += dot(glow[...].astype(BF), X[...], 0, 0)

    eye = sub == lane

    def y_copy(j, d):
        to = lax.rem(e + d, 4)
        return remote(mixs.at[j, to], mixr.at[j, d - 1], ys.at[j, d - 1], yr.at[j, d - 1], at_y(d))

    def combine(j):
        accm[...] = jnp.zeros_like(accm)

        @pl.loop(0, NX)
        def _(n):
            @pl.when(n != x)
            def _():
                remote(outb.at[j, n], outb.at[j, n], os_.at[j, 0], orr.at[j, n], sibling).wait_recv()

            coefs = info[j, pl.ds(32 + e * 8 + n * 2 + zh, 1), :]
            cf = jnp.sum(jnp.where(eye, coefs, 0.0), axis=1, keepdims=True)
            block = outb[j, n]
            accm[:, : D // 2] += cf * dot(PL_[j, n], block, 0, 0)
            accm[:, D // 2 :] += cf * dot(PR_[j, n], block, 0, 0)

        for yy in range(4):
            mixs[j, yy] = accm[:, yy * 512 : (yy + 1) * 512].astype(BF)
        for d in (2, 1, 3):
            y_copy(j, d).start()
        accown[j] = accm[:, pl.ds(pl.multiple_of(e * 512, 512), 512)]

    def home_copy(j, device):
        return remote(zsb.at[j - 1], zrb.at[j - 1], zs.at[j - 1], zr.at[j - 1], device)

    def send_home(j):
        for d in (1, 3, 2):
            y_copy(j, d).wait_recv()
        total = accown[j]
        for d in range(3):
            total = total + mixr[j, d].astype(F32)

        @pl.when(j == 0)
        def _():
            accown[0] = total

        @pl.when(j > 0)
        def _():
            zsb[j - 1] = total.astype(BF)
            home_copy(j, at_z(jnp.where(j == 3, 4, jnp.where(j == 2, 6, 2)))).start()

    @pl.loop(0, 4)
    def _(j):
        @pl.loop(0, NX)
        def _(n):
            @pl.when(n != x)
            def _():
                remote(rowsb.at[j, n], rowsb.at[j, n], rs.at[j, 0], rr.at[j, n], sibling).wait_recv()

        work(j)

        @pl.when(j >= 1)
        def _():
            combine(j - 1)

        @pl.when(j >= 2)
        def _():
            send_home(j - 2)

    gins[...] = gin[...].reshape(PARTS, LOWR, D).astype(BF)
    gouts[...] = gout[...].astype(BF)

    def gin_copy(d):
        k = lax.rem(mine + d, 8)
        return remote(gins.at[k], ginr.at[d - 1], gs.at[d - 1], gr.at[d - 1], in_group(k))

    def gout_copy(d):
        k = lax.rem(mine4 + d, 4)
        return remote(gouts.at[k], goutr.at[d - 1], hs.at[d - 1], hr.at[d - 1], in_group(pair * 4 + k))

    for d in range(1, 8):
        gin_copy(d).start()
    for d in range(1, 4):
        gout_copy(d).start()

    combine(3)
    send_home(2)
    send_home(3)

    for d in range(1, 8):
        gin_copy(d).wait_recv()
    for d in range(1, 4):
        gout_copy(d).wait_recv()
    total = gins[mine].astype(F32)
    for d in range(7):
        total = total + ginr[d].astype(F32)
    gin_o[...] = total
    total = gout[mine4]
    for d in range(3):
        total = total + goutr[d].astype(F32)
    gout_o[...] = total

    total = accown[0]
    for j in (1, 2, 3):
        home_copy(j, sibling).wait_recv()
        total = total + zrb[j - 1].astype(F32)
    mixed_o[...] = total.astype(BF)

    for j in (1, 2, 3):
        info_copy(j).wait_send()
        tz_copy(j).wait_send()
        home_copy(j, sibling).wait_send()
        for d in range(1, 4):
            ty_copy(j, d).wait_send()
    for d in range(1, 8):
        kz_copy(d).wait_send()
        wa_copy(d).wait_send()
        gin_copy(d).wait_send()
    for d in range(1, 4):
        kx_copy(d).wait_send()
        gout_copy(d).wait_send()
    for d in range(4):
        kc_copy(d).wait_send()
    for p in range(PIECES):
        w_copy(own(p), mine4, p, 0, neighbour).wait_send()
        w_copy(own(p), mine4, p, 1, sibling).wait_send()
        w_copy(slot(near4, p), near4, p, 2, sibling).wait_send()

    @pl.loop(0, 4)
    def _(j):
        for d in range(1, 4):
            y_copy(j, d).wait_send()

        @pl.loop(0, NX)
        def _(n):
            @pl.when(n != x)
            def _():
                row_copy(j, n).wait_send()
                remote(retb.at[j, n], outb.at[j, x], os_.at[j, n], orr.at[j, x], sibling).wait_send()


def run(queries, keys, values, hidden, cotangent, routes, route_weight, wgu, wd, ain, aout):
    vm = pl.BlockSpec(memory_space=pltpu.VMEM)
    hbm = pl.BlockSpec(memory_space=pl.ANY)
    dma = pltpu.SemaphoreType.DMA
    v = pltpu.VMEM
    return pl.pallas_call(
        kernel,
        out_shape=(
            jax.ShapeDtypeStruct((TOK, HEADS * HD), BF),
            jax.ShapeDtypeStruct((TOK, 512), BF),
            jax.ShapeDtypeStruct((LOWR, D), F32),
            jax.ShapeDtypeStruct((RANK, 2 * FF), F32),
        ),
        in_specs=[vm] * 7 + [hbm] * 4,
        out_specs=(vm,) * 4,
        scratch_shapes=[
            v((NX * NZ, 2, TOK, 2 * HD), BF),
            v((HEADS, HD, TOK), BF),
            v((HEADS, 8, TOK), F32),
            v((HEADS, 8, TOK), F32),
            v((HEADS, HD, TOK), F32),
            v((HALF, D, 2 * FF), BF),
            v((HALF, FF, D), BF),
            v((PARTS, LOWR, D), BF),
            v((HALF, RANK, 2 * FF), BF),
            v((HALF, 2 * RANK, 2 * FF), BF),
            v((4, NX, BLK, TOK), BF),
            v((4, NX, BLK, TOK), BF),
            v((4, 64, TOK), F32),
            v((64, D), BF),
            v((3, 4, 64, D), BF),
            v((4, NX, BLK, D), BF),
            v((4, NX, BLK, D), BF),
            v((ROWS, D), BF),
            v((ROWS, D), BF),
            v((ROWS, D), F32),
            v((ROWS, 2 * RANK), BF),
            v((ROWS, 2 * RANK), F32),
            v((PARTS * LOWR, D), F32),
            v((HALF, RANK, 2 * FF), F32),
            v((4, NX, BLK, D // 2), BF),
            v((4, NX, BLK, D // 2), BF),
            v((PARTS, LOWR, D), BF),
            v((HALF, RANK, 2 * FF), BF),
            v((7, LOWR, D), BF),
            v((3, RANK, 2 * FF), BF),
            v((TOK, D), F32),
            v((4, TOK, 512), F32),
            v((4, 4, TOK, 512), BF),
            v((4, 3, TOK, 512), BF),
            v((3, TOK, 512), BF),
            v((3, TOK, 512), BF),
            dma((3, PIECES)),
            dma((HALF, PIECES)),
            dma((PIECES + 1,)),
            dma((7,)),
            dma((7,)),
            dma((4, NX)),
            dma((4, NX)),
            dma((4, NX)),
            dma((4, NX)),
            dma((7,)),
            dma((7,)),
            dma((3,)),
            dma((3,)),
            dma((4, 3)),
            dma((4, 3)),
            dma((3,)),
            dma((3,)),
            dma((3,)),
            dma((3,)),
            dma((3, 3)),
            dma((3, 3)),
            dma((3,)),
            dma((3,)),
            dma((7,)),
            dma((7,)),
            dma((3,)),
            dma((3,)),
            dma((4,)),
            dma((4,)),
        ],
        compiler_params=pltpu.CompilerParams(
            collective_id=0, has_side_effects=True, vmem_limit_bytes=60 << 20
        ),
        cost_estimate=pl.CostEstimate(
            flops=16 << 30, bytes_accessed=32 << 20, transcendentals=8 << 20
        ),
        name="whole",
    )(queries, keys, values, hidden, cotangent, routes, route_weight, wgu, wd, ain, aout)


def local(
    queries, keys, values, hidden, cotangent, routes, route_weight,
    w_gate_up, w_down, adapter_in, adapter_out,
):
    context, mixed, gin, gout = run(
        queries, keys, values, hidden, cotangent, routes.T, route_weight.T,
        w_gate_up[0, 0], w_down[0, 0], adapter_in[0, 0].T, adapter_out[0, 0],
    )
    return (context, mixed, gin.T[None, None], gout[None, None])


def solution(mesh):
    return jax.shard_map(
        local,
        mesh=mesh,
        in_specs=(
            P("seq", "ep"),
            P("seq", "ep"),
            P("seq", "ep"),
            P("seq", None),
            P("seq", None),
            P("seq", None),
            P("seq", None),
            P("ep", "seq", None, None),
            P("ep", "seq", None, None),
            P("ep", "seq", None, None),
            P("ep", "seq", None, None),
        ),
        out_specs=(
            P("seq", "ep"),
            P("seq", "ep"),
            P("ep", "seq", None, None),
            P("ep", "seq", None, None),
        ),
        check_vma=False,
    )
```

```python
import jax
import jax.numpy as jnp
from jax import lax
from jax.experimental import pallas as pl
from jax.experimental.pallas import tpu as pltpu
from jax.sharding import PartitionSpec as P

BF = jnp.bfloat16
F32 = jnp.float32
MESH = pl.DeviceIdType.MESH

TOK = 128
D = 2048
HD = 128
HEADS = 8
FF = 192
BLK = 80
MAIN = 32
ROWS = 160
NX, NZ = 4, 8
PARTS = 8
LOWR = 16
RANK = 64
KEYS = 1024
SCALE = HD**-0.5 * 1.4426950408889634
PIECES = 4
HALF = 4
OFF = (0, 2, 6, 4)


def dot(a, b, ca, cb):
    return lax.dot_general(a, b, (((ca,), (cb,)), ((), ())), preferred_element_type=F32)


def kernel(
    queries, keys, values, hid, cot, routes, rw, wgu, wd, ain, aout,
    ctx_o, mixed_o, gin_o, gout_o,
    kvb, QT, top, den, num, WG, WD, WA, WB, WBB, PA, PL_, PR_, info, sl2, tk,
    sendb, rowsb, X, C, acc, low, glow, gin, gout,
    retb, outb, gins, gouts, ginr, goutr, accown, mixs, mixr, zsb, zrb,
    ws, wr, lw, was, war, rs, rr, os_, orr, gs, gr, hs, hr, ys, yr, zs, zr,
    tzs, tzr, tys, tyr, izs, izr, kzs, kzr, kxs, kxr, kcs, kcr,
):
    s = lax.axis_index("seq")
    e = lax.axis_index("ep")
    x = s // 16
    z = lax.rem(s // 2, 8)
    c = lax.rem(s, 2)
    zh = z // 4
    lz = lax.rem(z, 4)
    pair = lz // 2
    place = x * NZ + z
    mine = lz * 2 + c
    mine4 = lax.rem(lz, 2) * 2 + c

    def dev(xx, zz, cc):
        return ((xx * NZ + zz) * 2 + cc, e)

    def in_group(k):
        return dev(x, zh * 4 + k // 2, lax.rem(k, 2))

    def at_z(d):
        return dev(x, lax.rem(z + d, 8), c)

    def at_x(d):
        return dev(lax.rem(x + d, 4), z, c)

    def at_y(d):
        return (s, lax.rem(e + d, 4))

    sibling = dev(x, z, 1 - c)
    neighbour = dev(x, z + 1 - 2 * lax.rem(lz, 2), c)

    def remote(src, dst, send, recv, device):
        return pltpu.make_async_remote_copy(
            src_ref=src, dst_ref=dst, send_sem=send, recv_sem=recv, device_id=device, device_id_type=MESH
        )

    kvb[place, c, :, 0:HD] = keys[...]
    kvb[place, c, :, HD:] = values[...]
    for j in range(4):
        tk[0, j, 0:32] = hid[j * 32 : (j + 1) * 32]
        tk[0, j, 32:64] = cot[j * 32 : (j + 1) * 32]
    lane = lax.broadcasted_iota(jnp.int32, (TOK, TOK), 1)
    sub = lax.broadcasted_iota(jnp.int32, (TOK, TOK), 0)
    ids = lax.broadcasted_iota(jnp.int32, (32, TOK), 0)
    chosen = jnp.zeros((32, TOK), F32)
    coef = jnp.zeros((32, TOK), F32)
    for j in range(8):
        hit = routes[j : j + 1, :] == ids
        chosen = chosen + jnp.where(hit, 1.0, 0.0)
        coef = coef + jnp.where(hit, rw[j : j + 1, :], 0.0)
    before = jnp.where(sub < lane, 1.0, 0.0).astype(BF)
    info[0, 0:32] = jnp.where(chosen > 0.5, dot(chosen.astype(BF), before, 1, 0), 512.0)
    info[0, 32:64] = coef

    barrier = pltpu.get_barrier_semaphore()

    def greet(device):
        pl.semaphore_signal(barrier, inc=1, device_id=device, device_id_type=MESH)

    for d in range(1, 8):
        greet(at_z(d))
        greet(in_group(lax.rem(mine + d, 8)))
    for d in range(1, 4):
        greet(at_x(d))
        greet(at_y(d))
    pl.semaphore_wait(barrier, 20)

    def kz_copy(d):
        block = kvb.at[place, c]
        return remote(block, block, kzs.at[d - 1], kzr.at[d - 1], at_z(d))

    def kx_copy(d):
        block = kvb.at[pl.ds(x * NZ, NZ), c]
        return remote(block, block, kxs.at[d - 1], kxr.at[d - 1], at_x(d))

    def kc_copy(d):
        block = kvb.at[pl.ds(lax.rem(x + 4 - d, 4) * NZ, NZ), c]
        return remote(block, block, kcs.at[d], kcr.at[d], sibling)

    def tz_copy(j):
        return remote(tk.at[0, e], tk.at[j, e], tzs.at[j - 1], tzr.at[j - 1], at_z(8 - OFF[j]))

    def ty_copy(j, d):
        block = tk.at[j, e]
        return remote(block, block, tys.at[j - 1, d - 1], tyr.at[j - 1, d - 1], at_y(d))

    def info_copy(j):
        return remote(info.at[0], info.at[j], izs.at[j - 1], izr.at[j - 1], at_z(8 - OFF[j]))

    def slot(k, p):
        if p < 2:
            return WG.at[k, pl.ds(p * (D // 2), D // 2)]
        return (WD, WB)[p - 2].at[k]

    def own(p):
        if p < 2:
            return wgu.at[pl.ds(p * (D // 2), D // 2)]
        return (wd, aout)[p - 2]

    def w_copy(src, k, p, role, device):
        return remote(src, slot(k, p), ws.at[role, p], wr.at[k, p], device)

    def local_w(p):
        return pltpu.make_async_copy(own(p), slot(mine4, p), lw.at[p])

    def wa_copy(d):
        k = lax.rem(mine + d, 8)
        return remote(ain, WA.at[mine], was.at[d - 1], war.at[d - 1], in_group(k))

    local_wa = pltpu.make_async_copy(ain, WA.at[mine], lw.at[PIECES])
    near4 = lax.rem(mine4 + 2, 4)

    for j in (1, 2):
        info_copy(j).start()
        tz_copy(j).start()
    for p in range(PIECES):
        w_copy(own(p), mine4, p, 1, sibling).start()
        local_w(p).start()
    local_wa.start()

    row = lax.broadcasted_iota(jnp.int32, (BLK, 2 * TOK), 0)
    tail = row >= 2 * MAIN
    is_l = jnp.logical_or(row < MAIN, jnp.logical_and(tail, row < 2 * MAIN + 8))
    first = jnp.where(tail, row - MAIN, row).astype(F32)
    second = jnp.where(tail, row - MAIN - 8, row - MAIN).astype(F32)
    target_l = jnp.where(is_l, first, -1.0)
    target_r = jnp.where(is_l, -1.0, second)
    one_l = jnp.where(is_l, 1.0, 0.0)[:, :1]
    wide = lax.broadcasted_iota(jnp.int32, (BLK, 2 * TOK), 1)
    target_w = jnp.where(lax.rem(wide, 64) < 32, target_l, target_r)
    target_l = target_l[:, :TOK]
    target_r = target_r[:, :TOK]
    wide = lax.broadcasted_iota(jnp.int32, (TOK, 2 * TOK), 1)
    token = lax.broadcasted_iota(jnp.int32, (TOK, 2 * TOK), 0)
    spread = jnp.where((wide // 64) * 32 + lax.rem(wide, 32) == token, 1.0, 0.0).astype(BF)

    def row_copy(j, n):
        return remote(sendb.at[j, n], rowsb.at[j, x], rs.at[j, n], rr.at[j, x], dev(n, z, c))

    def dispatch(j):
        sl2[...] = dot(info[j, 0:32].astype(BF), spread, 1, 0)
        factor = []
        for n in range(NX):
            expert = e * 8 + n * 2 + zh
            slots = info[j, pl.ds(expert, 1), :]
            coefs = info[j, pl.ds(32 + expert, 1), :]
            p_l = jnp.where(slots == target_l, coefs, 0.0)
            p_r = jnp.where(slots == target_r, coefs, 0.0)
            factor.append(jnp.sum(p_r, axis=1, keepdims=True) + one_l)
            PL_[j, n] = p_l.astype(BF)
            PR_[j, n] = p_r.astype(BF)
            PA[n] = jnp.where(sl2[pl.ds(expert, 1), :] == target_w, 1.0, 0.0).astype(BF)
        for half in range(2):
            cols = slice(half * (D // 2), (half + 1) * (D // 2))
            picked = dot(PA[...].reshape(NX * BLK, 2 * TOK), tk[j, :, :, cols].reshape(2 * TOK, D // 2), 1, 0)
            for n in range(NX):
                block = (picked[n * BLK : (n + 1) * BLK] * factor[n]).astype(BF)

                @pl.when(n == x)
                def _():
                    rowsb[j, n, :, cols] = block

                @pl.when(n != x)
                def _():
                    sendb[j, n, :, cols] = block

        @pl.loop(0, NX)
        def _(n):
            @pl.when(n != x)
            def _():
                row_copy(j, n).start()

    def from_z(j):
        remote(tk.at[j, e], tk.at[j, e], tzs.at[j - 1], tzr.at[j - 1], sibling).wait_recv()
        remote(info.at[j], info.at[j], izs.at[j - 1], izr.at[j - 1], sibling).wait_recv()
        for d in (2, 1, 3):
            ty_copy(j, d).start()

    def more_sends():
        info_copy(3).start()
        tz_copy(3).start()
        for d in range(1, 8):
            wa_copy(d).start()
        for d in (4, 3, 5, 2, 6, 1, 7):
            kz_copy(d).start()
        for p in range(PIECES):
            w_copy(own(p), mine4, p, 0, neighbour).start()

    @pl.loop(0, 4)
    def _(j):
        @pl.when(j >= 1)
        def _():
            for d in (1, 3, 2):
                ty_copy(j, d).wait_recv()

            @pl.when(j < 3)
            def _():
                from_z(j + 1)

        dispatch(j)

        @pl.when(j == 0)
        def _():
            more_sends()
            from_z(1)

        @pl.when(j == 3)
        def _():
            for d in range(1, 8):
                kz_copy(d).wait_recv()
            for d in (2, 1, 3):
                kx_copy(d).start()
            kc_copy(0).start()

    for h in range(HEADS):
        QT[h] = queries[:, h * HD : (h + 1) * HD].astype(F32).T.astype(BF)
    top[...] = jnp.full_like(top, -1e30)
    den[...] = jnp.zeros_like(den)
    num[...] = jnp.zeros_like(num)
    gout[...] = jnp.zeros_like(gout)

    def absorb(block, masked):
        kv = kvb[pl.ds(block * (KEYS // 256), KEYS // 256)]
        ks = kv[..., :HD].reshape(KEYS, HD)
        vs = kv[..., HD:].reshape(KEYS, HD)
        if masked:
            kpos = block * KEYS + lax.broadcasted_iota(jnp.int32, (KEYS, TOK), 0)
            qpos = s * TOK + lax.broadcasted_iota(jnp.int32, (KEYS, TOK), 1)
            allowed = kpos <= qpos
        for h in range(HEADS):
            sc = dot(ks, QT[h], 1, 0)
            if masked:
                sc = jnp.where(allowed, sc, -1e30)
            old = top[h, 0:1]
            new = jnp.maximum(old, jnp.max(sc, axis=0, keepdims=True))
            factor = jnp.exp2((old - new) * SCALE)
            w = jnp.exp2((sc - new) * SCALE)
            den[h, 0:1] = den[h, 0:1] * factor + jnp.sum(w, axis=0, keepdims=True)
            num[h] = num[h] * factor + dot(vs, w.astype(BF), 0, 0)
            top[h, 0:1] = new

    full = s // (KEYS // TOK)

    lanes = lax.broadcasted_iota(jnp.int32, (RANK, 2 * FF), 1)

    def spread_wb(k):
        b = WB[k].astype(F32)
        WBB[k, pl.ds(0, RANK)] = jnp.where(lanes < FF, b, 0.0).astype(BF)
        WBB[k, pl.ds(RANK, RANK)] = jnp.where(lanes >= FF, b, 0.0).astype(BF)

    def prepare(i):
        for j in range(4):
            X[i, j * MAIN : (j + 1) * MAIN] = rowsb[i, j, 0:MAIN]
            C[i, j * MAIN : (j + 1) * MAIN] = rowsb[i, j, MAIN : 2 * MAIN]
        for j in range(2):
            t0 = rowsb[i, 2 * j, 2 * MAIN : BLK].astype(F32)
            t1 = rowsb[i, 2 * j + 1, 2 * MAIN : BLK].astype(F32)
            at = 4 * MAIN + 16 * j
            X[i, at : at + 16] = jnp.concatenate([t0[:8], t1[:8]], axis=0).astype(BF)
            C[i, at : at + 16] = jnp.concatenate([t0[8:], t1[8:]], axis=0).astype(BF)
        low[i] = dot(X[i], WA[...].reshape(PARTS * LOWR, D), 1, 1).astype(BF)
        glow[i] = jnp.zeros((ROWS, 2 * RANK), F32)
        acc[i] = jnp.zeros((ROWS, D), F32)

    def parts(i, base):
        @pl.loop(base, base + 2)
        def _(k):
            lo = low[i]
            pre = dot(X[i], WG[k], 1, 0) + dot(lo, WBB[k], 1, 0)
            g = pre[:, :FF]
            u = pre[:, FF:]
            back = dot(C[i], WD[k], 1, 1)
            sig = 1.0 / (1.0 + jnp.exp(-g))
            silu = g * sig
            acc[i] += dot((silu * u).astype(BF), WD[k], 1, 0)
            dg = back * u * sig * (1.0 + g * (1.0 - sig))
            du = back * silu
            dgu = jnp.concatenate([dg, du], axis=1).astype(BF)
            r = dot(lo, dgu, 0, 0)
            gout[k] += jnp.where(lanes < FF, r[:RANK], r[RANK:])
            glow[i] += dot(dgu, WBB[k], 1, 1)

    def give_back(i):
        for j in range(4):
            a = acc[i, j * MAIN : (j + 1) * MAIN].astype(BF)
            t = acc[i, 4 * MAIN + 8 * j : 4 * MAIN + 8 * j + 8]
            t = jnp.concatenate([t[:, : D // 2], t[:, D // 2 :]], axis=0).astype(BF)

            @pl.when(x == j)
            def _():
                outb[i, j, 0:MAIN] = a[:, : D // 2]
                outb[i, j, MAIN : 2 * MAIN] = a[:, D // 2 :]
                outb[i, j, 2 * MAIN : BLK] = t

            @pl.when(x != j)
            def _():
                retb[i, j, 0:MAIN] = a[:, : D // 2]
                retb[i, j, MAIN : 2 * MAIN] = a[:, D // 2 :]
                retb[i, j, 2 * MAIN : BLK] = t
                remote(retb.at[i, j], outb.at[i, x], os_.at[i, j], orr.at[i, x], dev(j, z, c)).start()


    def y_copy(j, d):
        to = lax.rem(e + d, 4)
        return remote(mixs.at[j, to], mixr.at[j, d - 1], ys.at[j, d - 1], yr.at[j, d - 1], at_y(d))

    def combine(j):
        @pl.loop(0, NX)
        def _(n):
            @pl.when(n != x)
            def _():
                remote(outb.at[j, n], outb.at[j, n], os_.at[j, 0], orr.at[j, n], sibling).wait_recv()

        for i, p in enumerate((PL_, PR_)):
            part = dot(p[j].reshape(NX * BLK, TOK), outb[j].reshape(NX * BLK, D // 2), 0, 0).astype(BF)
            mixs[j, 2 * i] = part[:, :512]
            mixs[j, 2 * i + 1] = part[:, 512:]
        for d in (2, 1, 3):
            y_copy(j, d).start()

    def home_copy(j, device):
        return remote(zsb.at[j - 1], zrb.at[j - 1], zs.at[j - 1], zr.at[j - 1], device)

    def send_home(j):
        for d in (1, 3, 2):
            y_copy(j, d).wait_recv()
        total = mixs[j, e].astype(F32)
        for d in range(3):
            total = total + mixr[j, d].astype(F32)

        @pl.when(j == 0)
        def _():
            accown[...] = total

        @pl.when(j > 0)
        def _():
            zsb[j - 1] = total.astype(BF)
            home_copy(j, at_z(jnp.where(j == 3, 4, jnp.where(j == 2, 6, 2)))).start()

    here = lax.rem(lz, 2) * 2
    there = 2 - here
    for p in range(PIECES):
        local_w(p).wait()
        w_copy(slot(here + 1 - c, p), here + 1 - c, p, 0, sibling).wait_recv()
    local_wa.wait()
    for d in range(1, 8):
        wa_copy(d).wait_recv()

    @pl.loop(here, here + 2)
    def _(k):
        spread_wb(k)

    @pl.loop(0, 4)
    def _(j):
        @pl.loop(0, NX)
        def _(n):
            @pl.when(n != x)
            def _():
                remote(rowsb.at[j, n], rowsb.at[j, n], rs.at[j, 0], rr.at[j, n], sibling).wait_recv()

        prepare(j)
        parts(j, here)

    for p in range(PIECES):
        w_copy(slot(near4, p), near4, p, 0, sibling).wait_recv()
        w_copy(slot(near4, p), near4, p, 2, sibling).start()
    for p in range(PIECES):
        w_copy(slot(there + 1 - c, p), there + 1 - c, p, 0, sibling).wait_recv()

    @pl.loop(there, there + 2)
    def _(k):
        spread_wb(k)

    @pl.loop(1, 5)
    def _(jj):
        j = lax.rem(jj, 4)
        parts(j, there)
        give_back(j)

    gin[...] = dot(glow[...].reshape(4 * ROWS, 2 * RANK).astype(BF), X[...].reshape(4 * ROWS, D), 0, 0)

    gins[...] = gin[...].reshape(PARTS, LOWR, D).astype(BF)
    gouts[...] = gout[...].astype(BF)

    def gin_copy(d):
        k = lax.rem(mine + d, 8)
        return remote(gins.at[k], ginr.at[d - 1], gs.at[d - 1], gr.at[d - 1], in_group(k))

    def gout_copy(d):
        k = lax.rem(mine4 + d, 4)
        return remote(gouts.at[k], goutr.at[d - 1], hs.at[d - 1], hr.at[d - 1], in_group(pair * 4 + k))

    for d in range(1, 8):
        gin_copy(d).start()
    for d in range(1, 4):
        gout_copy(d).start()

    for d in (1, 3, 2):
        kx_copy(d).wait_recv()
        kc_copy(d).start()
    for d in range(4):
        kc_copy(d).wait_recv()
    absorb(full, True)

    @pl.loop(0, 4)
    def _(jj):
        @pl.loop(full * jj // 4, full * (jj + 1) // 4)
        def _(t):
            absorb(t, False)

        combine(lax.rem(jj + 1, 4))

        @pl.when(jj >= 1)
        def _():
            send_home(jj)

    for h in range(HEADS):
        ctx_o[:, h * HD : (h + 1) * HD] = (num[h] / den[h, 0:1]).T.astype(BF)
    send_home(0)

    for d in range(1, 8):
        gin_copy(d).wait_recv()
    for d in range(1, 4):
        gout_copy(d).wait_recv()
    total = gins[mine].astype(F32)
    for d in range(7):
        total = total + ginr[d].astype(F32)
    gin_o[...] = total
    total = gout[mine4]
    for d in range(3):
        total = total + goutr[d].astype(F32)
    gout_o[...] = total

    total = accown[...]
    for j in (1, 2, 3):
        home_copy(j, sibling).wait_recv()
        total = total + zrb[j - 1].astype(F32)
    mixed_o[...] = total.astype(BF)

    for j in (1, 2, 3):
        info_copy(j).wait_send()
        tz_copy(j).wait_send()
        home_copy(j, sibling).wait_send()
        for d in range(1, 4):
            ty_copy(j, d).wait_send()
    for d in range(1, 8):
        kz_copy(d).wait_send()
        wa_copy(d).wait_send()
        gin_copy(d).wait_send()
    for d in range(1, 4):
        kx_copy(d).wait_send()
        gout_copy(d).wait_send()
    for d in range(4):
        kc_copy(d).wait_send()
    for p in range(PIECES):
        w_copy(own(p), mine4, p, 0, neighbour).wait_send()
        w_copy(own(p), mine4, p, 1, sibling).wait_send()
        w_copy(slot(near4, p), near4, p, 2, sibling).wait_send()

    @pl.loop(0, 4)
    def _(j):
        for d in range(1, 4):
            y_copy(j, d).wait_send()

        @pl.loop(0, NX)
        def _(n):
            @pl.when(n != x)
            def _():
                row_copy(j, n).wait_send()
                remote(retb.at[j, n], outb.at[j, x], os_.at[j, n], orr.at[j, x], sibling).wait_send()


def finish_kernel(*refs):
    half = len(refs) // 2
    for source, target in zip(refs[:half], refs[half:]):
        target[...] = source[...]


def finish(arrays):
    vm = pl.BlockSpec(memory_space=pltpu.VMEM)
    return pl.pallas_call(
        finish_kernel,
        out_shape=tuple(jax.ShapeDtypeStruct(a.shape, a.dtype) for a in arrays),
        in_specs=[vm] * len(arrays),
        out_specs=(vm,) * len(arrays),
        name="finish",
    )(*arrays)


def run(queries, keys, values, hidden, cotangent, routes, route_weight, wgu, wd, ain, aout):
    vm = pl.BlockSpec(memory_space=pltpu.VMEM)
    hbm = pl.BlockSpec(memory_space=pl.ANY)
    dma = pltpu.SemaphoreType.DMA
    v = pltpu.VMEM
    return pl.pallas_call(
        kernel,
        out_shape=(
            jax.ShapeDtypeStruct((TOK, HEADS * HD), BF),
            jax.ShapeDtypeStruct((TOK, 512), BF),
            jax.ShapeDtypeStruct((LOWR, D), F32),
            jax.ShapeDtypeStruct((RANK, 2 * FF), F32),
        ),
        in_specs=[vm] * 7 + [hbm] * 4,
        out_specs=(vm,) * 4,
        scratch_shapes=[
            v((NX * NZ, 2, TOK, 2 * HD), BF),
            v((HEADS, HD, TOK), BF),
            v((HEADS, 8, TOK), F32),
            v((HEADS, 8, TOK), F32),
            v((HEADS, HD, TOK), F32),
            v((HALF, D, 2 * FF), BF),
            v((HALF, FF, D), BF),
            v((PARTS, LOWR, D), BF),
            v((HALF, RANK, 2 * FF), BF),
            v((HALF, 2 * RANK, 2 * FF), BF),
            v((NX, BLK, 2 * TOK), BF),
            v((4, NX, BLK, TOK), BF),
            v((4, NX, BLK, TOK), BF),
            v((4, 64, TOK), F32),
            v((32, 2 * TOK), F32),
            v((4, 4, 64, D), BF),
            v((4, NX, BLK, D), BF),
            v((4, NX, BLK, D), BF),
            v((4, ROWS, D), BF),
            v((4, ROWS, D), BF),
            v((4, ROWS, D), F32),
            v((4, ROWS, 2 * RANK), BF),
            v((4, ROWS, 2 * RANK), F32),
            v((PARTS * LOWR, D), F32),
            v((HALF, RANK, 2 * FF), F32),
            v((4, NX, BLK, D // 2), BF),
            v((4, NX, BLK, D // 2), BF),
            v((PARTS, LOWR, D), BF),
            v((HALF, RANK, 2 * FF), BF),
            v((7, LOWR, D), BF),
            v((3, RANK, 2 * FF), BF),
            v((TOK, 512), F32),
            v((4, 4, TOK, 512), BF),
            v((4, 3, TOK, 512), BF),
            v((3, TOK, 512), BF),
            v((3, TOK, 512), BF),
            dma((3, PIECES)),
            dma((HALF, PIECES)),
            dma((PIECES + 1,)),
            dma((7,)),
            dma((7,)),
            dma((4, NX)),
            dma((4, NX)),
            dma((4, NX)),
            dma((4, NX)),
            dma((7,)),
            dma((7,)),
            dma((3,)),
            dma((3,)),
            dma((4, 3)),
            dma((4, 3)),
            dma((3,)),
            dma((3,)),
            dma((3,)),
            dma((3,)),
            dma((3, 3)),
            dma((3, 3)),
            dma((3,)),
            dma((3,)),
            dma((7,)),
            dma((7,)),
            dma((3,)),
            dma((3,)),
            dma((4,)),
            dma((4,)),
        ],
        compiler_params=pltpu.CompilerParams(
            collective_id=0, has_side_effects=True, vmem_limit_bytes=60 << 20
        ),
        cost_estimate=pl.CostEstimate(
            flops=16 << 30, bytes_accessed=32 << 20, transcendentals=8 << 20
        ),
        name="whole",
    )(queries, keys, values, hidden, cotangent, routes, route_weight, wgu, wd, ain, aout)


def local(
    queries, keys, values, hidden, cotangent, routes, route_weight,
    w_gate_up, w_down, adapter_in, adapter_out,
):
    outs = run(
        queries, keys, values, hidden, cotangent, routes.T, route_weight.T,
        w_gate_up[0, 0], w_down[0, 0], adapter_in[0, 0].T, adapter_out[0, 0],
    )
    context, mixed, gin, gout = finish(outs)
    return (context, mixed, gin.T[None, None], gout[None, None])


def solution(mesh):
    return jax.shard_map(
        local,
        mesh=mesh,
        in_specs=(
            P("seq", "ep"),
            P("seq", "ep"),
            P("seq", "ep"),
            P("seq", None),
            P("seq", None),
            P("seq", None),
            P("seq", None),
            P("ep", "seq", None, None),
            P("ep", "seq", None, None),
            P("ep", "seq", None, None),
            P("ep", "seq", None, None),
        ),
        out_specs=(
            P("seq", "ep"),
            P("seq", "ep"),
            P("ep", "seq", None, None),
            P("ep", "seq", None, None),
        ),
        check_vma=False,
    )
```

```python
import jax
import jax.numpy as jnp
from jax import lax
from jax.experimental import pallas as pl
from jax.experimental.pallas import tpu as pltpu
from jax.sharding import PartitionSpec as P

BF = jnp.bfloat16
F32 = jnp.float32
MESH = pl.DeviceIdType.MESH

TOK = 128
D = 2048
HD = 128
HEADS = 8
FF = 192
BLK = 80
MAIN = 32
ROWS = 160
NX, NZ = 4, 8
PARTS = 8
LOWR = 16
RANK = 64
KEYS = 1024
SCALE = HD**-0.5 * 1.4426950408889634
PIECES = 4
HALF = 4
OFF = (0, 2, 6, 4)


def dot(a, b, ca, cb):
    return lax.dot_general(a, b, (((ca,), (cb,)), ((), ())), preferred_element_type=F32)


def kernel(
    queries, keys, values, hid, cot, routes, rw, wgu, wd, ain, aout,
    ctx_o, mixed_o, gin_o, gout_o,
    kvb, QT, top, den, num, WG, WD, WA, WB, WBB, PA, PL_, PR_, info, sl2, tk,
    sendb, rowsb, X, C, acc, low, glow, gin, gout,
    retb, outb, gins, gouts, ginr, goutr, accown, mixs, mixr, zsb, zrb,
    ws, wr, lw, was, war, rs, rr, os_, orr, gs, gr, hs, hr, ys, yr, zs, zr,
    tzs, tzr, tys, tyr, izs, izr, kzs, kzr, kxs, kxr, kcs, kcr,
):
    s = lax.axis_index("seq")
    e = lax.axis_index("ep")
    x = s // 16
    z = lax.rem(s // 2, 8)
    c = lax.rem(s, 2)
    zh = z // 4
    lz = lax.rem(z, 4)
    pair = lz // 2
    place = x * NZ + z
    mine = lz * 2 + c
    mine4 = lax.rem(lz, 2) * 2 + c

    def dev(xx, zz, cc):
        return ((xx * NZ + zz) * 2 + cc, e)

    def in_group(k):
        return dev(x, zh * 4 + k // 2, lax.rem(k, 2))

    def at_z(d):
        return dev(x, lax.rem(z + d, 8), c)

    def at_x(d):
        return dev(lax.rem(x + d, 4), z, c)

    def at_y(d):
        return (s, lax.rem(e + d, 4))

    sibling = dev(x, z, 1 - c)
    neighbour = dev(x, z + 1 - 2 * lax.rem(lz, 2), c)

    def remote(src, dst, send, recv, device):
        return pltpu.make_async_remote_copy(
            src_ref=src, dst_ref=dst, send_sem=send, recv_sem=recv, device_id=device, device_id_type=MESH
        )

    kvb[place, c, :, 0:HD] = keys[...]
    kvb[place, c, :, HD:] = values[...]
    for j in range(4):
        tk[0, j, 0:32] = hid[j * 32 : (j + 1) * 32]
        tk[0, j, 32:64] = cot[j * 32 : (j + 1) * 32]
    lane = lax.broadcasted_iota(jnp.int32, (TOK, TOK), 1)
    sub = lax.broadcasted_iota(jnp.int32, (TOK, TOK), 0)
    ids = lax.broadcasted_iota(jnp.int32, (32, TOK), 0)
    chosen = jnp.zeros((32, TOK), F32)
    coef = jnp.zeros((32, TOK), F32)
    for j in range(8):
        hit = routes[j : j + 1, :] == ids
        chosen = chosen + jnp.where(hit, 1.0, 0.0)
        coef = coef + jnp.where(hit, rw[j : j + 1, :], 0.0)
    before = jnp.where(sub < lane, 1.0, 0.0).astype(BF)
    info[0, 0:32] = jnp.where(chosen > 0.5, dot(chosen.astype(BF), before, 1, 0), 512.0)
    info[0, 32:64] = coef

    barrier = pltpu.get_barrier_semaphore()

    def greet(device):
        pl.semaphore_signal(barrier, inc=1, device_id=device, device_id_type=MESH)

    for d in range(1, 8):
        greet(at_z(d))
        greet(in_group(lax.rem(mine + d, 8)))
    for d in range(1, 4):
        greet(at_x(d))
        greet(at_y(d))
    pl.semaphore_wait(barrier, 20)

    def kz_copy(d):
        block = kvb.at[place, c]
        return remote(block, block, kzs.at[d - 1], kzr.at[d - 1], at_z(d))

    def kx_copy(d):
        block = kvb.at[pl.ds(x * NZ, NZ), c]
        return remote(block, block, kxs.at[d - 1], kxr.at[d - 1], at_x(d))

    def kc_copy(d):
        block = kvb.at[pl.ds(lax.rem(x + 4 - d, 4) * NZ, NZ), c]
        return remote(block, block, kcs.at[d], kcr.at[d], sibling)

    def tz_copy(j):
        return remote(tk.at[0, e], tk.at[j, e], tzs.at[j - 1], tzr.at[j - 1], at_z(8 - OFF[j]))

    def ty_copy(j, d):
        block = tk.at[j, e]
        return remote(block, block, tys.at[j - 1, d - 1], tyr.at[j - 1, d - 1], at_y(d))

    def info_copy(j):
        return remote(info.at[0], info.at[j], izs.at[j - 1], izr.at[j - 1], at_z(8 - OFF[j]))

    def slot(k, p):
        if p < 2:
            return WG.at[k, pl.ds(p * (D // 2), D // 2)]
        return (WD, WB)[p - 2].at[k]

    def own(p):
        if p < 2:
            return wgu.at[pl.ds(p * (D // 2), D // 2)]
        return (wd, aout)[p - 2]

    def w_copy(src, k, p, role, device):
        return remote(src, slot(k, p), ws.at[role, p], wr.at[k, p], device)

    def local_w(p):
        return pltpu.make_async_copy(own(p), slot(mine4, p), lw.at[p])

    def wa_copy(d):
        k = lax.rem(mine + d, 8)
        return remote(ain, WA.at[mine], was.at[d - 1], war.at[d - 1], in_group(k))

    local_wa = pltpu.make_async_copy(ain, WA.at[mine], lw.at[PIECES])
    near4 = lax.rem(mine4 + 2, 4)

    for j in (1, 2):
        info_copy(j).start()
        tz_copy(j).start()
    for p in range(PIECES):
        w_copy(own(p), mine4, p, 1, sibling).start()
        local_w(p).start()
    local_wa.start()

    row = lax.broadcasted_iota(jnp.int32, (BLK, 2 * TOK), 0)
    tail = row >= 2 * MAIN
    is_l = jnp.logical_or(row < MAIN, jnp.logical_and(tail, row < 2 * MAIN + 8))
    first = jnp.where(tail, row - MAIN, row).astype(F32)
    second = jnp.where(tail, row - MAIN - 8, row - MAIN).astype(F32)
    target_l = jnp.where(is_l, first, -1.0)
    target_r = jnp.where(is_l, -1.0, second)
    one_l = jnp.where(is_l, 1.0, 0.0)[:, :1]
    wide = lax.broadcasted_iota(jnp.int32, (BLK, 2 * TOK), 1)
    target_w = jnp.where(lax.rem(wide, 64) < 32, target_l, target_r)
    target_l = target_l[:, :TOK]
    target_r = target_r[:, :TOK]
    wide = lax.broadcasted_iota(jnp.int32, (TOK, 2 * TOK), 1)
    token = lax.broadcasted_iota(jnp.int32, (TOK, 2 * TOK), 0)
    spread = jnp.where((wide // 64) * 32 + lax.rem(wide, 32) == token, 1.0, 0.0).astype(BF)

    def row_copy(j, n):
        return remote(sendb.at[j, n], rowsb.at[j, x], rs.at[j, n], rr.at[j, x], dev(n, z, c))

    def dispatch(j):
        sl2[...] = dot(info[j, 0:32].astype(BF), spread, 1, 0)
        factor = []
        for n in range(NX):
            expert = e * 8 + n * 2 + zh
            slots = info[j, pl.ds(expert, 1), :]
            coefs = info[j, pl.ds(32 + expert, 1), :]
            p_l = jnp.where(slots == target_l, coefs, 0.0)
            p_r = jnp.where(slots == target_r, coefs, 0.0)
            factor.append(jnp.sum(p_r, axis=1, keepdims=True) + one_l)
            PL_[j, n] = p_l.astype(BF)
            PR_[j, n] = p_r.astype(BF)
            PA[n] = jnp.where(sl2[pl.ds(expert, 1), :] == target_w, 1.0, 0.0).astype(BF)
        for half in range(2):
            cols = slice(half * (D // 2), (half + 1) * (D // 2))
            picked = dot(PA[...].reshape(NX * BLK, 2 * TOK), tk[j, :, :, cols].reshape(2 * TOK, D // 2), 1, 0)
            for n in range(NX):
                block = (picked[n * BLK : (n + 1) * BLK] * factor[n]).astype(BF)

                @pl.when(n == x)
                def _():
                    rowsb[j, n, :, cols] = block

                @pl.when(n != x)
                def _():
                    sendb[j, n, :, cols] = block

        @pl.loop(0, NX)
        def _(n):
            @pl.when(n != x)
            def _():
                row_copy(j, n).start()

    def from_z(j):
        remote(tk.at[j, e], tk.at[j, e], tzs.at[j - 1], tzr.at[j - 1], sibling).wait_recv()
        remote(info.at[j], info.at[j], izs.at[j - 1], izr.at[j - 1], sibling).wait_recv()
        for d in (2, 1, 3):
            ty_copy(j, d).start()

    def more_sends():
        info_copy(3).start()
        tz_copy(3).start()
        for d in range(1, 8):
            wa_copy(d).start()
        for d in (4, 3, 5, 2, 6, 1, 7):
            kz_copy(d).start()
        for p in range(PIECES):
            w_copy(own(p), mine4, p, 0, neighbour).start()

    @pl.loop(0, 4)
    def _(j):
        @pl.when(j >= 1)
        def _():
            for d in (1, 3, 2):
                ty_copy(j, d).wait_recv()

            @pl.when(j < 3)
            def _():
                from_z(j + 1)

        dispatch(j)

        @pl.when(j == 0)
        def _():
            more_sends()
            from_z(1)

        @pl.when(j == 3)
        def _():
            for d in range(1, 8):
                kz_copy(d).wait_recv()
            for d in (2, 1, 3):
                kx_copy(d).start()
            kc_copy(0).start()

    for h in range(HEADS):
        QT[h] = queries[:, h * HD : (h + 1) * HD].astype(F32).T.astype(BF)
    top[...] = jnp.full_like(top, -1e30)
    den[...] = jnp.zeros_like(den)
    num[...] = jnp.zeros_like(num)
    gout[...] = jnp.zeros_like(gout)

    def absorb(block, masked):
        kv = kvb[pl.ds(block * (KEYS // 256), KEYS // 256)]
        ks = kv[..., :HD].reshape(KEYS, HD)
        vs = kv[..., HD:].reshape(KEYS, HD)
        if masked:
            kpos = block * KEYS + lax.broadcasted_iota(jnp.int32, (KEYS, TOK), 0)
            qpos = s * TOK + lax.broadcasted_iota(jnp.int32, (KEYS, TOK), 1)
            allowed = kpos <= qpos
        for h in range(HEADS):
            sc = dot(ks, QT[h], 1, 0)
            if masked:
                sc = jnp.where(allowed, sc, -1e30)
            old = top[h, 0:1]
            new = jnp.maximum(old, jnp.max(sc, axis=0, keepdims=True))
            factor = jnp.exp2((old - new) * SCALE)
            w = jnp.exp2((sc - new) * SCALE)
            den[h, 0:1] = den[h, 0:1] * factor + jnp.sum(w, axis=0, keepdims=True)
            num[h] = num[h] * factor + dot(vs, w.astype(BF), 0, 0)
            top[h, 0:1] = new

    full = s // (KEYS // TOK)

    lanes = lax.broadcasted_iota(jnp.int32, (RANK, 2 * FF), 1)

    def spread_wb(k):
        b = WB[k].astype(F32)
        WBB[k, pl.ds(0, RANK)] = jnp.where(lanes < FF, b, 0.0).astype(BF)
        WBB[k, pl.ds(RANK, RANK)] = jnp.where(lanes >= FF, b, 0.0).astype(BF)

    def prepare(i):
        for j in range(4):
            X[i, j * MAIN : (j + 1) * MAIN] = rowsb[i, j, 0:MAIN]
            C[i, j * MAIN : (j + 1) * MAIN] = rowsb[i, j, MAIN : 2 * MAIN]
        for j in range(2):
            t0 = rowsb[i, 2 * j, 2 * MAIN : BLK].astype(F32)
            t1 = rowsb[i, 2 * j + 1, 2 * MAIN : BLK].astype(F32)
            at = 4 * MAIN + 16 * j
            X[i, at : at + 16] = jnp.concatenate([t0[:8], t1[:8]], axis=0).astype(BF)
            C[i, at : at + 16] = jnp.concatenate([t0[8:], t1[8:]], axis=0).astype(BF)
        low[i] = dot(X[i], WA[...].reshape(PARTS * LOWR, D), 1, 1).astype(BF)
        glow[i] = jnp.zeros((ROWS, 2 * RANK), F32)
        acc[i] = jnp.zeros((ROWS, D), F32)

    def parts(i, base):
        @pl.loop(base, base + 2)
        def _(k):
            lo = low[i]
            pre = dot(X[i], WG[k], 1, 0) + dot(lo, WBB[k], 1, 0)
            g = pre[:, :FF]
            u = pre[:, FF:]
            back = dot(C[i], WD[k], 1, 1)
            sig = 1.0 / (1.0 + jnp.exp(-g))
            silu = g * sig
            acc[i] += dot((silu * u).astype(BF), WD[k], 1, 0)
            dg = back * u * sig * (1.0 + g * (1.0 - sig))
            du = back * silu
            dgu = jnp.concatenate([dg, du], axis=1).astype(BF)
            r = dot(lo, dgu, 0, 0)
            gout[k] += jnp.where(lanes < FF, r[:RANK], r[RANK:])
            glow[i] += dot(dgu, WBB[k], 1, 1)

    def give_back(i):
        for j in range(4):
            a = acc[i, j * MAIN : (j + 1) * MAIN].astype(BF)
            t = acc[i, 4 * MAIN + 8 * j : 4 * MAIN + 8 * j + 8]
            t = jnp.concatenate([t[:, : D // 2], t[:, D // 2 :]], axis=0).astype(BF)

            @pl.when(x == j)
            def _():
                outb[i, j, 0:MAIN] = a[:, : D // 2]
                outb[i, j, MAIN : 2 * MAIN] = a[:, D // 2 :]
                outb[i, j, 2 * MAIN : BLK] = t

            @pl.when(x != j)
            def _():
                retb[i, j, 0:MAIN] = a[:, : D // 2]
                retb[i, j, MAIN : 2 * MAIN] = a[:, D // 2 :]
                retb[i, j, 2 * MAIN : BLK] = t
                remote(retb.at[i, j], outb.at[i, x], os_.at[i, j], orr.at[i, x], dev(j, z, c)).start()


    def y_copy(j, d):
        to = lax.rem(e + d, 4)
        return remote(mixs.at[j, to], mixr.at[j, d - 1], ys.at[j, d - 1], yr.at[j, d - 1], at_y(d))

    def combine(j):
        @pl.loop(0, NX)
        def _(n):
            @pl.when(n != x)
            def _():
                remote(outb.at[j, n], outb.at[j, n], os_.at[j, 0], orr.at[j, n], sibling).wait_recv()

        for i, p in enumerate((PL_, PR_)):
            part = dot(p[j].reshape(NX * BLK, TOK), outb[j].reshape(NX * BLK, D // 2), 0, 0).astype(BF)
            mixs[j, 2 * i] = part[:, :512]
            mixs[j, 2 * i + 1] = part[:, 512:]
        for d in (2, 1, 3):
            y_copy(j, d).start()

    def home_copy(j, device):
        return remote(zsb.at[j - 1], zrb.at[j - 1], zs.at[j - 1], zr.at[j - 1], device)

    def send_home(j):
        for d in (1, 3, 2):
            y_copy(j, d).wait_recv()
        total = mixs[j, e].astype(F32)
        for d in range(3):
            total = total + mixr[j, d].astype(F32)

        @pl.when(j == 0)
        def _():
            accown[...] = total

        @pl.when(j > 0)
        def _():
            zsb[j - 1] = total.astype(BF)
            home_copy(j, at_z(jnp.where(j == 3, 4, jnp.where(j == 2, 6, 2)))).start()

    here = lax.rem(lz, 2) * 2
    there = 2 - here
    for p in range(PIECES):
        local_w(p).wait()
        w_copy(slot(here + 1 - c, p), here + 1 - c, p, 0, sibling).wait_recv()
    local_wa.wait()
    for d in range(1, 8):
        wa_copy(d).wait_recv()

    @pl.loop(here, here + 2)
    def _(k):
        spread_wb(k)

    @pl.loop(0, 4)
    def _(j):
        @pl.loop(0, NX)
        def _(n):
            @pl.when(n != x)
            def _():
                remote(rowsb.at[j, n], rowsb.at[j, n], rs.at[j, 0], rr.at[j, n], sibling).wait_recv()

        prepare(j)
        parts(j, here)

    for p in range(PIECES):
        w_copy(slot(near4, p), near4, p, 0, sibling).wait_recv()
        w_copy(slot(near4, p), near4, p, 2, sibling).start()
    for p in range(PIECES):
        w_copy(slot(there + 1 - c, p), there + 1 - c, p, 0, sibling).wait_recv()

    @pl.loop(there, there + 2)
    def _(k):
        spread_wb(k)

    @pl.loop(1, 5)
    def _(jj):
        j = lax.rem(jj, 4)
        parts(j, there)
        give_back(j)

    gin[...] = dot(glow[...].reshape(4 * ROWS, 2 * RANK).astype(BF), X[...].reshape(4 * ROWS, D), 0, 0)

    gins[...] = gin[...].reshape(PARTS, LOWR, D).astype(BF)
    gouts[...] = gout[...].astype(BF)

    def gin_copy(d):
        k = lax.rem(mine + d, 8)
        return remote(gins.at[k], ginr.at[d - 1], gs.at[d - 1], gr.at[d - 1], in_group(k))

    def gout_copy(d):
        k = lax.rem(mine4 + d, 4)
        return remote(gouts.at[k], goutr.at[d - 1], hs.at[d - 1], hr.at[d - 1], in_group(pair * 4 + k))

    for d in range(1, 8):
        gin_copy(d).start()
    for d in range(1, 4):
        gout_copy(d).start()

    def keys_here():
        for d in (1, 3, 2):
            kx_copy(d).wait_recv()
            kc_copy(d).start()
        for d in range(4):
            kc_copy(d).wait_recv()

    @pl.loop(0, 4)
    def _(jj):
        combine(lax.rem(jj + 1, 4))

        @pl.when(jj == 0)
        def _():
            keys_here()
            absorb(full, True)

        @pl.when(jj >= 1)
        def _():
            send_home(jj)

        @pl.loop(full * jnp.minimum(jj, 3) // 3, full * jnp.minimum(jj + 1, 3) // 3)
        def _(t):
            absorb(t, False)

    for h in range(HEADS):
        ctx_o[:, h * HD : (h + 1) * HD] = (num[h] / den[h, 0:1]).T.astype(BF)
    send_home(0)

    for d in range(1, 8):
        gin_copy(d).wait_recv()
    for d in range(1, 4):
        gout_copy(d).wait_recv()
    total = gins[mine].astype(F32)
    for d in range(7):
        total = total + ginr[d].astype(F32)
    gin_o[...] = total
    total = gout[mine4]
    for d in range(3):
        total = total + goutr[d].astype(F32)
    gout_o[...] = total

    total = accown[...]
    for j in (1, 2, 3):
        home_copy(j, sibling).wait_recv()
        total = total + zrb[j - 1].astype(F32)
    mixed_o[...] = total.astype(BF)

    for j in (1, 2, 3):
        info_copy(j).wait_send()
        tz_copy(j).wait_send()
        home_copy(j, sibling).wait_send()
        for d in range(1, 4):
            ty_copy(j, d).wait_send()
    for d in range(1, 8):
        kz_copy(d).wait_send()
        wa_copy(d).wait_send()
        gin_copy(d).wait_send()
    for d in range(1, 4):
        kx_copy(d).wait_send()
        gout_copy(d).wait_send()
    for d in range(4):
        kc_copy(d).wait_send()
    for p in range(PIECES):
        w_copy(own(p), mine4, p, 0, neighbour).wait_send()
        w_copy(own(p), mine4, p, 1, sibling).wait_send()
        w_copy(slot(near4, p), near4, p, 2, sibling).wait_send()

    @pl.loop(0, 4)
    def _(j):
        for d in range(1, 4):
            y_copy(j, d).wait_send()

        @pl.loop(0, NX)
        def _(n):
            @pl.when(n != x)
            def _():
                row_copy(j, n).wait_send()
                remote(retb.at[j, n], outb.at[j, x], os_.at[j, n], orr.at[j, x], sibling).wait_send()


def finish_kernel(*refs):
    half = len(refs) // 2
    for source, target in zip(refs[:half], refs[half:]):
        target[...] = source[...]


def finish(arrays):
    vm = pl.BlockSpec(memory_space=pltpu.VMEM)
    return pl.pallas_call(
        finish_kernel,
        out_shape=tuple(jax.ShapeDtypeStruct(a.shape, a.dtype) for a in arrays),
        in_specs=[vm] * len(arrays),
        out_specs=(vm,) * len(arrays),
        name="finish",
    )(*arrays)


def run(queries, keys, values, hidden, cotangent, routes, route_weight, wgu, wd, ain, aout):
    vm = pl.BlockSpec(memory_space=pltpu.VMEM)
    hbm = pl.BlockSpec(memory_space=pl.ANY)
    dma = pltpu.SemaphoreType.DMA
    v = pltpu.VMEM
    return pl.pallas_call(
        kernel,
        out_shape=(
            jax.ShapeDtypeStruct((TOK, HEADS * HD), BF),
            jax.ShapeDtypeStruct((TOK, 512), BF),
            jax.ShapeDtypeStruct((LOWR, D), F32),
            jax.ShapeDtypeStruct((RANK, 2 * FF), F32),
        ),
        in_specs=[vm] * 7 + [hbm] * 4,
        out_specs=(vm,) * 4,
        scratch_shapes=[
            v((NX * NZ, 2, TOK, 2 * HD), BF),
            v((HEADS, HD, TOK), BF),
            v((HEADS, 8, TOK), F32),
            v((HEADS, 8, TOK), F32),
            v((HEADS, HD, TOK), F32),
            v((HALF, D, 2 * FF), BF),
            v((HALF, FF, D), BF),
            v((PARTS, LOWR, D), BF),
            v((HALF, RANK, 2 * FF), BF),
            v((HALF, 2 * RANK, 2 * FF), BF),
            v((NX, BLK, 2 * TOK), BF),
            v((4, NX, BLK, TOK), BF),
            v((4, NX, BLK, TOK), BF),
            v((4, 64, TOK), F32),
            v((32, 2 * TOK), F32),
            v((4, 4, 64, D), BF),
            v((4, NX, BLK, D), BF),
            v((4, NX, BLK, D), BF),
            v((4, ROWS, D), BF),
            v((4, ROWS, D), BF),
            v((4, ROWS, D), F32),
            v((4, ROWS, 2 * RANK), BF),
            v((4, ROWS, 2 * RANK), F32),
            v((PARTS * LOWR, D), F32),
            v((HALF, RANK, 2 * FF), F32),
            v((4, NX, BLK, D // 2), BF),
            v((4, NX, BLK, D // 2), BF),
            v((PARTS, LOWR, D), BF),
            v((HALF, RANK, 2 * FF), BF),
            v((7, LOWR, D), BF),
            v((3, RANK, 2 * FF), BF),
            v((TOK, 512), F32),
            v((4, 4, TOK, 512), BF),
            v((4, 3, TOK, 512), BF),
            v((3, TOK, 512), BF),
            v((3, TOK, 512), BF),
            dma((3, PIECES)),
            dma((HALF, PIECES)),
            dma((PIECES + 1,)),
            dma((7,)),
            dma((7,)),
            dma((4, NX)),
            dma((4, NX)),
            dma((4, NX)),
            dma((4, NX)),
            dma((7,)),
            dma((7,)),
            dma((3,)),
            dma((3,)),
            dma((4, 3)),
            dma((4, 3)),
            dma((3,)),
            dma((3,)),
            dma((3,)),
            dma((3,)),
            dma((3, 3)),
            dma((3, 3)),
            dma((3,)),
            dma((3,)),
            dma((7,)),
            dma((7,)),
            dma((3,)),
            dma((3,)),
            dma((4,)),
            dma((4,)),
        ],
        compiler_params=pltpu.CompilerParams(
            collective_id=0, has_side_effects=True, vmem_limit_bytes=60 << 20
        ),
        cost_estimate=pl.CostEstimate(
            flops=16 << 30, bytes_accessed=32 << 20, transcendentals=8 << 20
        ),
        name="whole",
    )(queries, keys, values, hidden, cotangent, routes, route_weight, wgu, wd, ain, aout)


def local(
    queries, keys, values, hidden, cotangent, routes, route_weight,
    w_gate_up, w_down, adapter_in, adapter_out,
):
    outs = run(
        queries, keys, values, hidden, cotangent, routes.T, route_weight.T,
        w_gate_up[0, 0], w_down[0, 0], adapter_in[0, 0].T, adapter_out[0, 0],
    )
    context, mixed, gin, gout = finish(outs)
    return (context, mixed, gin.T[None, None], gout[None, None])


def solution(mesh):
    return jax.shard_map(
        local,
        mesh=mesh,
        in_specs=(
            P("seq", "ep"),
            P("seq", "ep"),
            P("seq", "ep"),
            P("seq", None),
            P("seq", None),
            P("seq", None),
            P("seq", None),
            P("ep", "seq", None, None),
            P("ep", "seq", None, None),
            P("ep", "seq", None, None),
            P("ep", "seq", None, None),
        ),
        out_specs=(
            P("seq", "ep"),
            P("seq", "ep"),
            P("ep", "seq", None, None),
            P("ep", "seq", None, None),
        ),
        check_vma=False,
    )
```
